256 devices in a mesh: dom: 64 (over x, y_hi, z), col: 4 (over y_lo, core).
Axes of the slice: x: 4, y: 4 (y_hi: 2, y_lo: 2; y = y_hi * 2 + y_lo), z: 8, core: 2. Of those that a mesh axis runs over, the one named last changes fastest.
Arguments:
- l_values: bfloat16 [2304, 64, 448], P(('dom', 'col')), may hold values from -0.375 to 0.375
- s_values: bfloat16 [2304, 64, 448], P(('dom', 'col')), may hold values from -6 to 6
- h_values: bfloat16 [2304, 64, 448], P(('dom', 'col')), may hold values from -0.375 to 0.375
- pattern: int32 [2304, 7], replicated, may hold values 0 or 1
Outputs:
- kernel: bfloat16 [2304, 64, 448], P(('dom', 'col'))
- gradient: bfloat16 [2304, 64, 448], P(('dom', 'col'))
The draws below stay inside these ranges and needn't reach their ends.
All inputs are finite; a program needn't handle non-finite values.
Results may differ from the reference program's by a relative error of at most 0.0064.
Values may be sent and summed in bfloat16 or wider, within the bound.
No kernel may reach another device: no remote copies, remote signals or barrier semaphores. Data moves between devices by JAX's collectives and lax.ppermute only.
A program may use at most 128 MiB of HBM per device.

```python
import jax
import jax.numpy as jnp

BLK = 64
W = 7
NB = 2304


def set_ends(values, own_key, smallest, largest):
    dims = values.shape
    place = [jax.random.randint(jax.random.fold_in(own_key, axis), (), 0, dims[axis]) for axis in range(len(dims))]
    values = values.at[tuple(place)].set(smallest)
    longest = dims.index(max(dims))
    place[longest] = (place[longest] + 1) % dims[longest]
    return values.at[tuple(place)].set(largest)


def block_scale(rng, extent, cuts, smallest, largest):
    def one(dim, blocks):
        heights = jax.random.uniform(jax.random.fold_in(jax.random.fold_in(rng, 6), dim), (blocks,), jnp.float32, smallest / len(cuts), largest / len(cuts))
        return jnp.repeat(jnp.exp(heights), extent[dim] // blocks).reshape((-1,) + (1,) * (len(extent) - dim - 1))

    loudness = one(*cuts[0])
    for cut in cuts[1:]:
        loudness = loudness * one(*cut)
    return loudness


def normal_values(key, extent, scale, reach, split=(), dtype=jnp.bfloat16):
    entries = scale * jax.random.normal(key, extent, jnp.float32)
    if split:
        entries = entries * block_scale(key, extent, split, -0.22, 0.18)
    return jnp.clip(entries, -reach, reach).astype(dtype)


def setup_inputs(seed: int = 0) -> dict:
    streams_of = jax.random.split(jax.random.key(seed), 5)
    return {
        "l_values": normal_values(streams_of[0], (NB, BLK, W * BLK), (BLK * W // 2) ** -0.5, 0.375, ((0, 256),)),
        "s_values": normal_values(streams_of[1], (NB, BLK, W * BLK), 1.0, 6.0, ((0, 256),)),
        "h_values": normal_values(streams_of[2], (NB, BLK, W * BLK), (BLK * W // 2) ** -0.5, 0.375, ((0, 256),)),
        "pattern": set_ends((jax.random.randint(streams_of[3], (NB, W), 0, 4) < 3).astype(jnp.int32), jax.random.fold_in(streams_of[3], 1), 0, 1),
    }


def truncated(left_matrix, right_matrix, pattern):
    block_rows, block_size, row_width = left_matrix.shape
    slot_count = row_width // block_size
    reach_len = (slot_count - 1) // 2
    left_four = left_matrix.reshape(block_rows, block_size, slot_count, block_size)
    right_four = right_matrix.reshape(block_rows, block_size, slot_count, block_size)
    outputs = []
    for target in range(slot_count):
        first = max(0, target - reach_len)
        last = min(slot_count - 1, target + reach_len)
        gathered = []
        for inner in range(first, last + 1):
            rolled = jnp.roll(right_four[:, :, target - inner + reach_len, :], reach_len - inner, axis=0)
            gathered.append(rolled)
        stacked = jnp.stack(gathered, axis=1).astype(jnp.float32)
        left_part = left_four[:, :, first:last + 1, :].astype(jnp.float32)
        outputs.append(jnp.einsum("irtm,itmn->irn", left_part, stacked))
    accumulated = jnp.stack(outputs, axis=2)
    keep_mask = pattern.astype(jnp.float32)[:, None, :, None]
    return (accumulated * keep_mask).reshape(block_rows, block_size, row_width)


def masked(values, pattern):
    block_rows, block_size, row_width = values.shape
    slot_count = row_width // block_size
    four = values.reshape(block_rows, block_size, slot_count, block_size)
    return (four * pattern.astype(jnp.bfloat16)[:, None, :, None]).reshape(values.shape)


def reference(l_values, s_values, h_values, pattern):
    block_rows, block_size, row_width = l_values.shape
    slot_count = row_width // block_size
    reach_len = (slot_count - 1) // 2
    l_masked = masked(l_values, pattern)
    s_masked = masked(s_values, pattern)
    h_masked = masked(h_values, pattern)
    product_ls = truncated(l_masked, s_masked, pattern).astype(jnp.bfloat16)
    lsl_term = truncated(product_ls, l_masked, pattern).astype(jnp.bfloat16)
    quintic = truncated(lsl_term, product_ls, pattern)
    kernel = (3.0 * lsl_term.astype(jnp.float32) - 2.0 * quintic).astype(jnp.bfloat16)
    hls_term = truncated(h_masked, product_ls, pattern).astype(jnp.bfloat16)
    hls_four = hls_term.reshape(block_rows, block_size, slot_count, block_size)
    pieces = []
    for offset in range(slot_count):
        source = hls_four[:, :, 2 * reach_len - offset, :]
        rolled = jnp.roll(source, reach_len - offset, axis=0)
        pieces.append(jnp.transpose(rolled, (0, 2, 1)))
    mirrored = jnp.stack(pieces, axis=2).reshape(block_rows, block_size, row_width)
    keep_mask = pattern.astype(jnp.float32)[:, None, :, None]
    summed = (hls_term.astype(jnp.float32) + mirrored.astype(jnp.float32)).reshape(block_rows, block_size, slot_count, block_size)
    gradient = (summed * keep_mask).reshape(block_rows, block_size, row_width).astype(jnp.bfloat16)
    return kernel, gradient
```

```python
import jax
import jax.numpy as jnp
from jax import lax
from jax.experimental import pallas as pl
from jax.experimental.pallas import tpu as pltpu
from jax.sharding import PartitionSpec as P

BLK = 64
SLOTS = 7
REACH = 3
ROWS = 9
LANES = 512
AXES = ("dom", "col")


def shift_of(q):
    return 1 - q % 2


def column_of(q, position):
    return q - REACH + position - shift_of(q)


def halo_plan(side):
    if side == 0:
        rows = {"l": range(-3, 0), "s": range(-6, 0), "h": range(-3, 0)}
    else:
        rows = {"l": range(9, 12), "s": range(9, 15), "h": range(9, 12)}
    full, low, high = [], [], []
    for name in ("s", "l", "h"):
        for q in rows[name]:
            for chunk in range(4):
                need = []
                for position in (2 * chunk, 2 * chunk + 1):
                    slot = position - shift_of(q)
                    column = column_of(q, position)
                    inside = 0 <= slot < SLOTS
                    if name != "l":
                        inside = inside and (column >= -3 if side == 0 else column <= 11)
                    need.append(inside)
                a, b = (name, q, 2 * chunk), (name, q, 2 * chunk + 1)
                if all(need):
                    full.append((a, b))
                elif need[0]:
                    low.append(a)
                elif need[1]:
                    high.append(b)
    while low and high:
        full.append((low.pop(), high.pop()))
    rest = low + high
    while rest:
        a = rest.pop()
        full.append((a, rest.pop() if rest else None))
    return full


PLANS = (halo_plan(0), halo_plan(1))
CHUNKS = len(PLANS[0])


def pack_kernel(cross, l_hbm, s_hbm, h_hbm, out_ref, l_buf, s_buf, h_buf, sems):
    core = lax.rem(lax.axis_index("col"), 2)
    right = core if cross else 1 - core
    copies = [
        pltpu.make_async_copy(s_hbm.at[pl.ds(3 * right, 6)], s_buf, sems.at[0]),
        pltpu.make_async_copy(l_hbm.at[pl.ds(6 * right, 3)], l_buf, sems.at[1]),
        pltpu.make_async_copy(h_hbm.at[pl.ds(6 * right, 3)], h_buf, sems.at[2]),
    ]
    for copy in copies:
        copy.start()
    for copy in copies:
        copy.wait()
    bufs = {"l": l_buf, "s": s_buf, "h": h_buf}

    def write(side):
        def block(name, q, position):
            slot = position - shift_of(q)
            row = q - 9 if side == 1 else (q + 6 if name == "s" else q + 3)
            return bufs[name], row, slot

        for n, (a, b) in enumerate(PLANS[side]):
            ref, row, slot = block(*a)
            if b is not None and a[:2] == b[:2] and b[2] == a[2] + 1:
                chunk = ref[row, :, slot * BLK : (slot + 2) * BLK]
            else:
                first = ref[row, :, slot * BLK : (slot + 1) * BLK]
                if b is None:
                    second = jnp.zeros_like(first)
                else:
                    ref, row, slot = block(*b)
                    second = ref[row, :, slot * BLK : (slot + 1) * BLK]
                chunk = jnp.concatenate([first, second], axis=1)
            out_ref[n * BLK : (n + 1) * BLK, :] = chunk

    pl.when(right == 1)(lambda: write(0))
    pl.when(right == 0)(lambda: write(1))


def pack(cross, l_values, s_values, h_values):
    return pl.pallas_call(
        lambda *refs: pack_kernel(cross, *refs),
        out_shape=jax.ShapeDtypeStruct((CHUNKS * BLK, 128), jnp.bfloat16),
        in_specs=[pl.BlockSpec(memory_space=pl.ANY)] * 3,
        out_specs=pl.BlockSpec(memory_space=pltpu.VMEM),
        scratch_shapes=[
            pltpu.VMEM((3, BLK, SLOTS * BLK), jnp.bfloat16),
            pltpu.VMEM((6, BLK, SLOTS * BLK), jnp.bfloat16),
            pltpu.VMEM((3, BLK, SLOTS * BLK), jnp.bfloat16),
            pltpu.SemaphoreType.DMA((3,)),
        ],
        name="pack_cross" if cross else "pack_chip",
    )(l_values, s_values, h_values)


RANGE = {"s": (-6, 16), "l": (-4, 13), "h": (-3, 13), "p": (-4, 13), "g": (-4, 14), "t": (-1, 9)}
MASK_FIRST = -6
OFFSET = (-2, -1, -1, 0, 0, 1, 1, 2)


def rows_of(name, q, count=1):
    first = (q - RANGE[name][0]) * BLK
    return slice(first, first + count * BLK)


def compute_kernel(
    l_ref, s_ref, h_ref, cross_ref, chip_ref, mask_ref, kernel_ref, gradient_ref, *scratch
):
    st = dict(zip(("s", "l", "h", "p", "g", "t"), scratch))
    core = lax.rem(lax.axis_index("col"), 2)
    zero_chunk = jnp.zeros((BLK, 128), jnp.bfloat16)

    def mask_row(q, first, last):
        row = q - MASK_FIRST
        return mask_ref[row : row + 1, first * 128 : last * 128]

    def zero_row(name, q):
        st[name][rows_of(name, q), :] = jnp.zeros((BLK, LANES), jnp.bfloat16)

    for name, q in (("s", 15), ("l", -4), ("l", 12), ("h", 12), ("p", -4), ("g", -4), ("g", 13)):
        zero_row(name, q)

    for name, ref in (("s", s_ref), ("l", l_ref), ("h", h_ref)):
        for q in range(ROWS):
            values = ref[q]
            pad = jnp.zeros((BLK, BLK), jnp.bfloat16)
            parts = [pad, values] if shift_of(q) else [values, pad]
            stored = jnp.concatenate(parts, axis=1)
            st[name][rows_of(name, q), :] = stored * mask_row(q, 0, 4).astype(jnp.bfloat16)

    def unpack(side, ref):
        content = {}
        for n, (a, b) in enumerate(PLANS[side]):
            for half, key in ((0, a), (1, b)):
                if key is not None:
                    content[key] = (n, half)
        halo = {"s": range(-6, 0), "l": range(-3, 0), "h": range(-3, 0)}
        if side == 1:
            halo = {"s": range(9, 15), "l": range(9, 12), "h": range(9, 12)}
        for name in halo:
            for q in halo[name]:
                for chunk in range(4):
                    places = [content.get((name, q, 2 * chunk + half)) for half in (0, 1)]
                    if places == [None, None]:
                        values = zero_chunk
                    else:
                        n, half = next(p for p in places if p is not None)
                        if places[0] is not None and places[1] == (n, 1) and places[0] == (n, 0):
                            values = ref[n * BLK : (n + 1) * BLK, :]
                        else:
                            parts = []
                            for place in places:
                                if place is None:
                                    parts.append(jnp.zeros((BLK, BLK), jnp.bfloat16))
                                else:
                                    n, half = place
                                    parts.append(
                                        ref[n * BLK : (n + 1) * BLK, half * BLK : (half + 1) * BLK]
                                    )
                            values = jnp.concatenate(parts, axis=1)
                        values = values * mask_row(q, chunk, chunk + 1).astype(jnp.bfloat16)
                    st[name][rows_of(name, q), chunk * 128 : (chunk + 1) * 128] = values

    @pl.when(core == 1)
    def _():
        unpack(0, chip_ref)
        unpack(1, cross_ref)

    @pl.when(core == 0)
    def _():
        unpack(0, cross_ref)
        unpack(1, chip_ref)

    def product(left, right, q, first, last, depth=(0, 8)):
        lhs = st[left][rows_of(left, q, 2), depth[0] * BLK : depth[1] * BLK]
        slabs = []
        for r in range(*depth):
            parts = []
            for chunk in range(first, last):
                source = chunk - OFFSET[r]
                if 0 <= source < 4:
                    rows = rows_of(right, q - REACH + r)
                    parts.append(st[right][rows, source * 128 : (source + 1) * 128])
                else:
                    parts.append(zero_chunk)
            slabs.append(jnp.concatenate(parts, axis=1))
        rhs = jnp.concatenate(slabs, axis=0)
        return jnp.dot(lhs, rhs, preferred_element_type=jnp.float32)

    def pair_mask(q, first, last):
        width = (last - first) * 128
        return jnp.concatenate(
            [jnp.broadcast_to(mask_row(q + k, first, last), (BLK, width)) for k in (0, 1)], axis=0
        )

    def store_product(target, left, right, q, pieces, depth=(0, 8)):
        for first, last in pieces:
            values = product(left, right, q, first, last, depth) * pair_mask(q, first, last)
            st[target][rows_of(target, q, 2), first * 128 : last * 128] = values.astype(
                jnp.bfloat16
            )

    halves = ((0, 2), (2, 4))
    for q in range(-3, 13, 2):
        pieces = halves
        if q == -3:
            pieces = ((1, 2), (2, 4))
        elif q == 9:
            pieces = ((0, 2), (2, 3))
        elif q == 11:
            pieces = ((0, 2),)
        store_product("p", "l", "s", q, pieces)
    for q, chunk in ((-3, 0), (9, 3), (11, 2), (11, 3)):
        st["p"][rows_of("p", q, 2), chunk * 128 : (chunk + 1) * 128] = jnp.zeros(
            (2 * BLK, 128), jnp.bfloat16
        )

    for q in range(-1, 9, 2):
        store_product("t", "p", "l", q, halves)
    for q in range(-1, 9, 2):
        values = []
        for first, last in halves:
            quintic = product("t", "p", q, first, last) * pair_mask(q, first, last)
            lsl = st["t"][rows_of("t", q, 2), first * 128 : last * 128].astype(jnp.float32)
            values.append((3.0 * lsl - 2.0 * quintic).astype(jnp.bfloat16))
        values = jnp.concatenate(values, axis=1)
        if q >= 0:
            kernel_ref[q] = values[:BLK, : SLOTS * BLK]
        kernel_ref[q + 1] = values[BLK:, BLK:]

    store_product("g", "h", "p", -3, ((3, 4),), (2, 8))
    for q in range(-1, 9, 2):
        store_product("g", "h", "p", q, halves)
    store_product("g", "h", "p", 9, ((0, 2),), (0, 6))
    store_product("g", "h", "p", 11, ((0, 1),), (0, 4))

    def stored_chunk(q, chunk):
        return st["g"][rows_of("g", q), chunk * 128 : (chunk + 1) * 128].astype(jnp.float32)

    for pair in range(5):
        mirrored = {}
        for step in range(-2, 3):
            upper = zero_chunk.astype(jnp.float32)
            lower = upper
            if step >= -1:
                upper = stored_chunk(2 * (pair + step), 2 - step)
            if step <= 1:
                lower = stored_chunk(2 * (pair + step) + 1, 1 - step)
            mirrored[step] = jnp.transpose(jnp.concatenate([upper, lower], axis=0))
        for k in (0, 1):
            q = 2 * pair + k
            if q >= ROWS:
                continue
            chunks = []
            for chunk in range(4):
                other = mirrored[chunk - 2 + k][k * BLK : (k + 1) * BLK]
                summed = (stored_chunk(q, chunk) + other) * mask_row(q, chunk, chunk + 1)
                chunks.append(summed.astype(jnp.bfloat16))
            values = jnp.concatenate(chunks, axis=1)
            gradient_ref[q] = values[:, : SLOTS * BLK] if k else values[:, BLK:]


def compute(l_values, s_values, h_values, cross, chip, mask):
    vmem = pl.BlockSpec(memory_space=pltpu.VMEM)
    out = jax.ShapeDtypeStruct(l_values.shape, jnp.bfloat16)
    return pl.pallas_call(
        compute_kernel,
        out_shape=(out, out),
        in_specs=[vmem] * 6,
        out_specs=(vmem, vmem),
        scratch_shapes=[
            pltpu.VMEM(((RANGE[name][1] - RANGE[name][0]) * BLK, LANES), jnp.bfloat16)
            for name in ("s", "l", "h", "p", "g", "t")
        ],
        compiler_params=pltpu.CompilerParams(vmem_limit_bytes=48 * 1024 * 1024),
        name="compute",
    )(l_values, s_values, h_values, cross, chip, mask)


def local_mask(pattern):
    device = lax.axis_index(AXES)
    turned = pattern.T
    around = jnp.concatenate([turned[:, -6:], turned, turned[:, :7]], axis=1)
    near = lax.dynamic_slice(around, (0, device * ROWS), (SLOTS, 22)).T.astype(jnp.float32)
    even = jnp.pad(near, ((0, 0), (1, 0)))
    odd = jnp.pad(near, ((0, 0), (0, 1)))
    stored = jnp.where(jnp.arange(22)[:, None] % 2 == 0, even, odd)
    return jnp.broadcast_to(stored[:, :, None], (22, 8, BLK)).reshape(22, LANES)


def shards(l_values, s_values, h_values, pattern):
    count = lax.axis_size(AXES)
    cross_pairs, chip_pairs = [], []
    for i in range(0, count, 2):
        j = (i - 1) % count
        cross_pairs += [(i, j), (j, i)]
        chip_pairs += [(i, i + 1), (i + 1, i)]
    cross = lax.ppermute(pack(True, l_values, s_values, h_values), AXES, cross_pairs)
    chip = lax.ppermute(pack(False, l_values, s_values, h_values), AXES, chip_pairs)
    mask = local_mask(pattern)
    return compute(l_values, s_values, h_values, cross, chip, mask)


def solution(mesh):
    rows = P(AXES, None, None)
    return jax.shard_map(
        shards,
        mesh=mesh,
        in_specs=(rows, rows, rows, P()),
        out_specs=(rows, rows),
        check_vma=False,
    )
```

```python
import jax
import jax.numpy as jnp
from jax import lax
from jax.experimental import pallas as pl
from jax.experimental.pallas import tpu as pltpu
from jax.sharding import PartitionSpec as P

BLK = 64
SLOTS = 7
REACH = 3
ROWS = 9
LANES = 512
AXES = ("dom", "col")


def shift_of(q):
    return 1 - q % 2


def column_of(q, position):
    return q - REACH + position - shift_of(q)


def halo_plan(side):
    if side == 0:
        rows = {"l": range(-3, 0), "s": range(-6, 0), "h": range(-3, 0)}
    else:
        rows = {"l": range(9, 12), "s": range(9, 15), "h": range(9, 12)}
    full, low, high = [], [], []
    for name in ("s", "l", "h"):
        for q in rows[name]:
            for chunk in range(4):
                need = []
                for position in (2 * chunk, 2 * chunk + 1):
                    slot = position - shift_of(q)
                    column = column_of(q, position)
                    inside = 0 <= slot < SLOTS
                    if name != "l":
                        inside = inside and (column >= -3 if side == 0 else column <= 11)
                    need.append(inside)
                a, b = (name, q, 2 * chunk), (name, q, 2 * chunk + 1)
                if all(need):
                    full.append((a, b))
                elif need[0]:
                    low.append(a)
                elif need[1]:
                    high.append(b)
    while low and high:
        full.append((low.pop(), high.pop()))
    rest = low + high
    while rest:
        a = rest.pop()
        full.append((a, rest.pop() if rest else None))
    return full


PLANS = (halo_plan(0), halo_plan(1))
CHUNKS = len(PLANS[0])
MASK_FIRST, MASK_ROWS = -6, 22
CHIP_PARTS = (CHUNKS // 2, CHUNKS - CHUNKS // 2)


def write_halo(side, block, out_refs):
    chunks = []
    for a, b in PLANS[side]:
        ref, row, lane = block(*a)
        if b is not None and a[:2] == b[:2] and b[2] == a[2] + 1:
            chunks.append(ref[row, :, lane : lane + 2 * BLK])
            continue
        first = ref[row, :, lane : lane + BLK]
        second = jnp.zeros_like(first)
        if b is not None:
            ref, row, lane = block(*b)
            second = ref[row, :, lane : lane + BLK]
        chunks.append(jnp.concatenate([first, second], axis=1))
    for out_ref in out_refs:
        for n in range(out_ref.shape[0] // BLK):
            out_ref[n * BLK : (n + 1) * BLK, :] = chunks.pop(0)


def sender_block(refs, side, first):
    def block(name, q, position):
        row = q - ROWS if side == 1 else q + ROWS
        return refs[name], row - first[name], (position - shift_of(q)) * BLK

    return block


def pack_cross_kernel(l_hbm, s_hbm, h_hbm, out_ref, l_buf, s_buf, h_buf, sems):
    core = lax.rem(lax.axis_index("col"), 2)
    copies = [
        pltpu.make_async_copy(s_hbm.at[pl.ds(3 * core, 6)], s_buf, sems.at[0]),
        pltpu.make_async_copy(l_hbm.at[pl.ds(6 * core, 3)], l_buf, sems.at[1]),
        pltpu.make_async_copy(h_hbm.at[pl.ds(6 * core, 3)], h_buf, sems.at[2]),
    ]
    for copy in copies:
        copy.start()
    for copy in copies:
        copy.wait()
    bufs = {"l": l_buf, "s": s_buf, "h": h_buf}
    last = sender_block(bufs, 0, {"l": 6, "s": 3, "h": 6})
    first = sender_block(bufs, 1, {"l": 0, "s": 0, "h": 0})
    pl.when(core == 1)(lambda: write_halo(0, last, (out_ref,)))
    pl.when(core == 0)(lambda: write_halo(1, first, (out_ref,)))


def pack_cross(l_values, s_values, h_values):
    hbm = pl.BlockSpec(memory_space=pltpu.HBM)
    return pl.pallas_call(
        pack_cross_kernel,
        out_shape=pltpu.VMEM((CHUNKS * BLK, 128), jnp.bfloat16),
        in_specs=[hbm] * 3,
        out_specs=pl.BlockSpec(memory_space=pltpu.VMEM),
        scratch_shapes=[
            pltpu.VMEM((3, BLK, SLOTS * BLK), jnp.bfloat16),
            pltpu.VMEM((6, BLK, SLOTS * BLK), jnp.bfloat16),
            pltpu.VMEM((3, BLK, SLOTS * BLK), jnp.bfloat16),
            pltpu.SemaphoreType.DMA((3,)),
        ],
        cost_estimate=pl.CostEstimate(flops=1, bytes_accessed=1, transcendentals=0),
        name="pack_cross",
    )(l_values, s_values, h_values)


def write_mask(pattern_ref, mask_ref):
    count, total = mask_ref.shape[0], pattern_ref.shape[1]
    device = lax.axis_index("dom") * lax.axis_size("col") + lax.axis_index("col")
    first = device * ROWS + MASK_FIRST + total
    wanted = lax.rem(first + lax.broadcasted_iota(jnp.int32, (count, total), 0), total)
    index = lax.broadcasted_iota(jnp.int32, (count, total), 1)
    picked = (wanted == index).astype(jnp.float32).astype(jnp.bfloat16)
    pattern = pattern_ref[...].astype(jnp.float32).astype(jnp.bfloat16)
    near = lax.dot_general(
        picked, pattern, (((1,), (1,)), ((), ())), preferred_element_type=jnp.float32
    )
    even = lax.rem(lax.broadcasted_iota(jnp.int32, (count, 1), 0), 2) == 0
    zero = jnp.zeros((count, 1), jnp.float32)
    slots = [zero] + [near[:, s : s + 1] for s in range(SLOTS)] + [zero]
    places = [jnp.where(even, slots[p], slots[p + 1]) for p in range(8)]
    low = lax.broadcasted_iota(jnp.int32, (count, 128), 1) < BLK
    for chunk in range(4):
        mask_ref[:, chunk * 128 : (chunk + 1) * 128] = jnp.where(
            low, places[2 * chunk], places[2 * chunk + 1]
        )


def pack_chip_kernel(l_ref, s_ref, h_ref, pattern_ref, after_ref, *out_refs):
    del after_ref
    *out_refs, mask_ref = out_refs
    write_mask(pattern_ref, mask_ref)
    core = lax.rem(lax.axis_index("col"), 2)
    refs = {"l": l_ref, "s": s_ref, "h": h_ref}
    whole = {"l": 0, "s": 0, "h": 0}
    pl.when(core == 0)(lambda: write_halo(0, sender_block(refs, 0, whole), out_refs))
    pl.when(core == 1)(lambda: write_halo(1, sender_block(refs, 1, whole), out_refs))


def pack_chip(l_values, s_values, h_values, turned, after):
    vmem = pl.BlockSpec(memory_space=pltpu.VMEM)
    return pl.pallas_call(
        pack_chip_kernel,
        out_shape=tuple(pltpu.VMEM((n * BLK, 128), jnp.bfloat16) for n in CHIP_PARTS)
        + (pltpu.VMEM((MASK_ROWS, LANES), jnp.float32),),
        in_specs=[vmem] * 5,
        out_specs=(vmem,) * (len(CHIP_PARTS) + 1),
        compiler_params=pltpu.CompilerParams(vmem_limit_bytes=8 * 1024 * 1024),
        cost_estimate=pl.CostEstimate(flops=1, bytes_accessed=1, transcendentals=0),
        name="pack_chip",
    )(l_values, s_values, h_values, turned, after)


NAMES = ("s", "l", "h", "p", "t", "g")
RANGE = {"s": (-6, 16), "l": (-4, 13), "h": (-3, 13), "p": (-4, 13), "t": (-1, 9), "g": (-3, 13)}
OFFSET = (-2, -1, -1, 0, 0, 1, 1, 2)
HALVES = ((0, 2), (2, 4))
HALO = (
    {"s": range(-6, 0), "l": range(-3, 0), "h": range(-3, 0)},
    {"s": range(9, 15), "l": range(9, 12), "h": range(9, 12)},
)
ZERO_ROWS = ((("l", -4), ("p", -4)), (("s", 15), ("l", 12), ("h", 12)))
ZERO_CHUNKS = (((-3, 0),), ((9, 3), (11, 2), (11, 3)))
LATE = (
    {"p": (-3, -1, 1), "t": (-1, 1), "g": (-3, -1, 1, 3, 5)},
    {"p": (5, 7, 9, 11), "t": (5, 7), "g": (1, 3, 5, 7, 9, 11)},
)
EARLY = (
    {"p": (3, 5, 7, 9, 11), "t": (3, 5, 7), "g": (7, 9, 11)},
    {"p": (-3, -1, 1, 3), "t": (-1, 1, 3), "g": (-3, -1)},
)


def rows_of(name, q, count=1):
    first = (q - RANGE[name][0]) * BLK
    return slice(first, first + count * BLK)


def is_late(core, name, q):
    if name in ("s", "l", "h"):
        return q < 0 if core == 0 else q >= ROWS
    group = q if q % 2 else q - 1
    if name == "p" and group < -3:
        return core == 0
    return group in LATE[core][name]


class Stored:
    def __init__(self, core, early, late, mask_ref):
        self.core, self.early, self.late, self.mask_ref = core, early, late, mask_ref

    def ref(self, name, q):
        use_late = self.late is not None and is_late(self.core, name, q)
        return (self.late if use_late else self.early)[name]

    def get(self, name, q, first=0, last=4):
        return self.ref(name, q)[rows_of(name, q), first * 128 : last * 128]

    def put(self, name, q, values, first=0, last=4):
        self.ref(name, q)[rows_of(name, q), first * 128 : last * 128] = values

    def mask(self, q, first, last):
        row = q - MASK_FIRST
        return self.mask_ref[row : row + 1, first * 128 : last * 128]

    def pair_mask(self, q, first, last):
        shape = (BLK, (last - first) * 128)
        return jnp.concatenate(
            [jnp.broadcast_to(self.mask(q + k, first, last), shape) for k in (0, 1)], axis=0
        )

    def own_rows(self, refs):
        pad = jnp.zeros((BLK, BLK), jnp.bfloat16)
        for name, ref in refs.items():
            for q in range(ROWS):
                values = ref[q]
                parts = [pad, values] if shift_of(q) else [values, pad]
                stored = jnp.concatenate(parts, axis=1)
                self.put(name, q, stored * self.mask(q, 0, 4).astype(jnp.bfloat16))

    def unpack(self, side, refs):
        pad = jnp.zeros((BLK, BLK), jnp.bfloat16)
        content = {}
        for n, keys in enumerate(PLANS[side]):
            for half, key in enumerate(keys):
                if key is not None:
                    content[key] = (n, half)

        def piece(n, first, last):
            for ref in refs:
                if n < ref.shape[0] // BLK:
                    break
                n -= ref.shape[0] // BLK
            return ref[n * BLK : (n + 1) * BLK, first * BLK : last * BLK]

        for name, rows in HALO[side].items():
            for q in rows:
                for chunk in range(4):
                    a, b = (content.get((name, q, 2 * chunk + half)) for half in (0, 1))
                    if a is None and b is None:
                        values = jnp.zeros((BLK, 128), jnp.bfloat16)
                    else:
                        if a is not None and b is not None and a[0] == b[0]:
                            values = piece(a[0], 0, 2)
                        else:
                            values = jnp.concatenate(
                                [pad if p is None else piece(p[0], p[1], p[1] + 1) for p in (a, b)],
                                axis=1,
                            )
                        values = values * self.mask(q, chunk, chunk + 1).astype(jnp.bfloat16)
                    self.put(name, q, values, chunk, chunk + 1)
        for name, q in ZERO_ROWS[side]:
            self.put(name, q, jnp.zeros((BLK, LANES), jnp.bfloat16))
        for q, chunk in ZERO_CHUNKS[side]:
            for k in (0, 1):
                self.put("p", q + k, jnp.zeros((BLK, 128), jnp.bfloat16), chunk, chunk + 1)

    def product(self, left, right, q, first, last, depth=(0, 8)):
        lhs = jnp.concatenate([self.get(left, q + k) for k in (0, 1)], axis=0)
        lhs = lhs[:, depth[0] * BLK : depth[1] * BLK]
        slabs = []
        for r in range(*depth):
            parts = []
            for chunk in range(first, last):
                source = chunk - OFFSET[r]
                if 0 <= source < 4:
                    parts.append(self.get(right, q - REACH + r, source, source + 1))
                else:
                    parts.append(jnp.zeros((BLK, 128), jnp.bfloat16))
            slabs.append(jnp.concatenate(parts, axis=1))
        rhs = jnp.concatenate(slabs, axis=0)
        return jnp.dot(lhs, rhs, preferred_element_type=jnp.float32)

    def put_product(self, target, left, right, q, pieces=HALVES, depth=(0, 8)):
        for first, last in pieces:
            values = self.product(left, right, q, first, last, depth)
            values = (values * self.pair_mask(q, first, last)).astype(jnp.bfloat16)
            self.ref(target, q)[rows_of(target, q, 2), first * 128 : last * 128] = values

    def product_ls(self, q):
        pieces = {-3: ((1, 2), (2, 4)), 9: ((0, 2), (2, 3)), 11: ((0, 2),)}.get(q, HALVES)
        self.put_product("p", "l", "s", q, pieces)

    def lsl_term(self, q):
        self.put_product("t", "p", "l", q)

    def hls_term(self, q):
        pieces, depth = {
            -3: (((3, 4),), (2, 8)),
            9: (((0, 2),), (0, 6)),
            11: (((0, 1),), (0, 4)),
        }.get(q, (HALVES, (0, 8)))
        self.put_product("g", "h", "p", q, pieces, depth)

    def kernel_rows(self, q, out_ref):
        values = []
        for first, last in HALVES:
            quintic = self.product("t", "p", q, first, last) * self.pair_mask(q, first, last)
            lsl = self.ref("t", q)[rows_of("t", q, 2), first * 128 : last * 128]
            values.append((3.0 * lsl.astype(jnp.float32) - 2.0 * quintic).astype(jnp.bfloat16))
        values = jnp.concatenate(values, axis=1)
        if q >= 0:
            out_ref[q] = values[:BLK, : SLOTS * BLK]
        out_ref[q + 1] = values[BLK:, BLK:]

    def gradient_rows(self, pair, out_ref):
        rows = [2 * pair + k for k in (0, 1) if 2 * pair + k < ROWS]
        zero = jnp.zeros((BLK, 128), jnp.bfloat16)
        mirrored = {}
        for step in range(-2, 3 if len(rows) == 2 else 2):
            upper = lower = zero
            if step >= -1:
                upper = self.get("g", 2 * (pair + step), 2 - step, 3 - step)
            if step <= 1:
                lower = self.get("g", 2 * (pair + step) + 1, 1 - step, 2 - step)
            mirrored[step] = jnp.transpose(jnp.concatenate([upper, lower], axis=0))
        for k, q in enumerate(rows):
            chunks = []
            for chunk in range(4):
                other = mirrored[chunk - 2 + k][k * BLK : (k + 1) * BLK].astype(jnp.float32)
                own = self.get("g", q, chunk, chunk + 1).astype(jnp.float32)
                summed = (own + other) * self.mask(q, chunk, chunk + 1)
                chunks.append(summed.astype(jnp.bfloat16))
            values = jnp.concatenate(chunks, axis=1)
            out_ref[q] = values[:, : SLOTS * BLK] if k else values[:, BLK:]


def early_kernel(l_ref, s_ref, h_ref, chip_a_ref, chip_b_ref, mask_ref, *outs):
    core = lax.rem(lax.axis_index("col"), 2)
    early = dict(zip(NAMES, outs))

    def run(which):
        st = Stored(which, early, None, mask_ref)
        st.own_rows({"s": s_ref, "l": l_ref, "h": h_ref})
        st.unpack(1 - which, (chip_a_ref, chip_b_ref))
        for q in EARLY[which]["p"]:
            st.product_ls(q)
        for q in EARLY[which]["t"]:
            st.lsl_term(q)
        for q in EARLY[which]["g"]:
            st.hls_term(q)

    pl.when(core == 0)(lambda: run(0))
    pl.when(core == 1)(lambda: run(1))


def stored_types():
    return [
        pltpu.VMEM(((RANGE[name][1] - RANGE[name][0]) * BLK, LANES), jnp.bfloat16)
        for name in NAMES
    ]


def compute_early(l_values, s_values, h_values, chip, mask):
    vmem = pl.BlockSpec(memory_space=pltpu.VMEM)
    return pl.pallas_call(
        early_kernel,
        out_shape=tuple(stored_types()),
        in_specs=[vmem] * 6,
        out_specs=(vmem,) * len(NAMES),
        compiler_params=pltpu.CompilerParams(vmem_limit_bytes=16 * 1024 * 1024),
        cost_estimate=pl.CostEstimate(flops=1, bytes_accessed=1, transcendentals=0),
        name="early",
    )(l_values, s_values, h_values, *chip, mask)


def late_kernel(cross_ref, mask_ref, *refs):
    early = dict(zip(NAMES, refs[:6]))
    kernel_hbm, gradient_hbm = refs[6:8]
    late = dict(zip(NAMES, refs[8:14]))
    kernel_buf, gradient_buf, sems = refs[14:]
    core = lax.rem(lax.axis_index("col"), 2)

    def run(which):
        st = Stored(which, early, late, mask_ref)
        copies = []

        def send(buf, hbm, first, count):
            copy = pltpu.make_async_copy(
                buf.at[first : first + count], hbm.at[first : first + count], sems.at[len(copies)]
            )
            copy.start()
            copies.append(copy)

        def kernel_rows(q):
            st.kernel_rows(q, kernel_buf)
            first = max(q, 0)
            send(kernel_buf, kernel_hbm, first, q + 2 - first)

        def gradient_rows(pair):
            st.gradient_rows(pair, gradient_buf)
            send(gradient_buf, gradient_hbm, 2 * pair, min(2, ROWS - 2 * pair))

        kernel_rows(7 if which == 0 else -1)
        st.unpack(which, (cross_ref,))
        for q in LATE[which]["p"]:
            st.product_ls(q)
        for q in LATE[which]["g"]:
            st.hls_term(q)
        for q in LATE[which]["t"]:
            st.lsl_term(q)
        order = (-1, 1, 3, 5) if which == 0 else (7, 5, 3, 1)
        for pair in range(5):
            gradient_rows(pair)
            if pair < 4:
                kernel_rows(order[pair])
        for copy in copies:
            copy.wait()

    pl.when(core == 0)(lambda: run(0))
    pl.when(core == 1)(lambda: run(1))


def compute_late(cross, mask, early):
    vmem = pl.BlockSpec(memory_space=pltpu.VMEM)
    hbm = pl.BlockSpec(memory_space=pl.ANY)
    out = jax.ShapeDtypeStruct((ROWS, BLK, SLOTS * BLK), jnp.bfloat16)
    buf = pltpu.VMEM((ROWS, BLK, SLOTS * BLK), jnp.bfloat16)
    return pl.pallas_call(
        late_kernel,
        out_shape=(out, out),
        in_specs=[vmem] * (2 + len(NAMES)),
        out_specs=(hbm, hbm),
        scratch_shapes=stored_types() + [buf, buf, pltpu.SemaphoreType.DMA((10,))],
        compiler_params=pltpu.CompilerParams(vmem_limit_bytes=16 * 1024 * 1024),
        name="late",
    )(cross, mask, *early)


def shards(l_values, s_values, h_values, pattern):
    count = lax.axis_size(AXES)
    cross_pairs, chip_pairs = [], []
    for i in range(0, count, 2):
        j = (i - 1) % count
        cross_pairs += [(i, j), (j, i)]
        chip_pairs += [(i, i + 1), (i + 1, i)]
    cross_out = pack_cross(l_values, s_values, h_values)
    cross = lax.ppermute(cross_out, AXES, cross_pairs)
    *chip_out, mask = pack_chip(l_values, s_values, h_values, pattern.T, cross_out)
    chip = [lax.ppermute(part, AXES, chip_pairs) for part in chip_out]
    early = compute_early(l_values, s_values, h_values, chip, mask)
    return compute_late(cross, mask, early)


def solution(mesh):
    rows = P(AXES, None, None)
    return jax.shard_map(
        shards,
        mesh=mesh,
        in_specs=(rows, rows, rows, P()),
        out_specs=(rows, rows),
        check_vma=False,
    )
```

```python
import functools

import jax
import jax.numpy as jnp
from jax import lax
from jax.experimental import pallas as pl
from jax.experimental.pallas import tpu as pltpu
from jax.sharding import PartitionSpec as P

BLK = 64
SLOTS = 7
REACH = 3
ROWS = 9
LANES = 512
AXES = ("dom", "col")


def shift_of(q):
    return 1 - q % 2


def column_of(q, position):
    return q - REACH + position - shift_of(q)


def halo_plan(side):
    if side == 0:
        rows = {"l": range(-3, 0), "s": range(-6, 0), "h": range(-3, 0)}
    else:
        rows = {"l": range(9, 12), "s": range(9, 15), "h": range(9, 12)}
    full, low, high = [], [], []
    for name in ("s", "l", "h"):
        for q in rows[name]:
            for chunk in range(4):
                need = []
                for position in (2 * chunk, 2 * chunk + 1):
                    slot = position - shift_of(q)
                    column = column_of(q, position)
                    inside = 0 <= slot < SLOTS
                    if name != "l":
                        inside = inside and (column >= -3 if side == 0 else column <= 11)
                    need.append(inside)
                a, b = (name, q, 2 * chunk), (name, q, 2 * chunk + 1)
                if all(need):
                    full.append((a, b))
                elif need[0]:
                    low.append(a)
                elif need[1]:
                    high.append(b)
    while low and high:
        full.append((low.pop(), high.pop()))
    rest = low + high
    while rest:
        a = rest.pop()
        full.append((a, rest.pop() if rest else None))
    return full


PLANS = (halo_plan(0), halo_plan(1))
CHUNKS = len(PLANS[0])
PACKED = CHUNKS * BLK - BLK // 2
CHIP_PARTS = (CHUNKS // 2 * BLK, PACKED - CHUNKS // 2 * BLK)
MASK_FIRST, MASK_ROWS = -6, 22


def write_halo(side, block, out_refs):
    for n, (a, b) in enumerate(PLANS[side]):
        ref, row, lane = block(*a)
        if b is None:
            only = ref[row, :, lane : lane + BLK]
            chunk = jnp.concatenate([only[: BLK // 2], only[BLK // 2 :]], axis=1)
        elif a[:2] == b[:2] and b[2] == a[2] + 1:
            chunk = ref[row, :, lane : lane + 2 * BLK]
        else:
            first = ref[row, :, lane : lane + BLK]
            ref, row, lane = block(*b)
            second = ref[row, :, lane : lane + BLK]
            chunk = jnp.concatenate([first, second], axis=1)
        place = n * BLK
        for out_ref in out_refs:
            if place < out_ref.shape[0]:
                break
            place -= out_ref.shape[0]
        out_ref[place : place + chunk.shape[0], :] = chunk


def sender_block(refs, side, first):
    def block(name, q, position):
        row = q - ROWS if side == 1 else q + ROWS
        return refs[name], row - first[name], (position - shift_of(q)) * BLK

    return block


def pack_cross_kernel(l_hbm, s_hbm, h_hbm, out_ref, l_buf, s_buf, h_buf, sems):
    core = lax.rem(lax.axis_index("col"), 2)
    copies = [
        pltpu.make_async_copy(s_hbm.at[pl.ds(3 * core, 6)], s_buf, sems.at[0]),
        pltpu.make_async_copy(l_hbm.at[pl.ds(6 * core, 3)], l_buf, sems.at[1]),
        pltpu.make_async_copy(h_hbm.at[pl.ds(6 * core, 3)], h_buf, sems.at[2]),
    ]
    for copy in copies:
        copy.start()
    bufs = {"l": l_buf, "s": s_buf, "h": h_buf}
    last = sender_block(bufs, 0, {"l": 6, "s": 3, "h": 6})
    first = sender_block(bufs, 1, {"l": 0, "s": 0, "h": 0})
    for copy in copies:
        copy.wait()
    pl.when(core == 1)(lambda: write_halo(0, last, (out_ref,)))
    pl.when(core == 0)(lambda: write_halo(1, first, (out_ref,)))


def pack_cross(l_values, s_values, h_values):
    hbm = pl.BlockSpec(memory_space=pltpu.HBM)
    return pl.pallas_call(
        pack_cross_kernel,
        out_shape=pltpu.VMEM((PACKED, 128), jnp.bfloat16),
        in_specs=[hbm] * 3,
        out_specs=pl.BlockSpec(memory_space=pltpu.VMEM),
        scratch_shapes=[
            pltpu.VMEM((3, BLK, SLOTS * BLK), jnp.bfloat16),
            pltpu.VMEM((6, BLK, SLOTS * BLK), jnp.bfloat16),
            pltpu.VMEM((3, BLK, SLOTS * BLK), jnp.bfloat16),
            pltpu.SemaphoreType.DMA((3,)),
        ],
        cost_estimate=pl.CostEstimate(flops=1, bytes_accessed=1, transcendentals=0),
        name="pack_cross",
    )(l_values, s_values, h_values)


def write_mask(pattern_ref, mask_ref):
    count, total = mask_ref.shape[0], pattern_ref.shape[1]
    device = lax.axis_index("dom") * lax.axis_size("col") + lax.axis_index("col")
    first = device * ROWS + MASK_FIRST + total
    wanted = lax.rem(first + lax.broadcasted_iota(jnp.int32, (count, total), 0), total)
    index = lax.broadcasted_iota(jnp.int32, (count, total), 1)
    picked = (wanted == index).astype(jnp.float32).astype(jnp.bfloat16)
    pattern = pattern_ref[...].astype(jnp.float32).astype(jnp.bfloat16)
    near = lax.dot_general(
        picked, pattern, (((1,), (1,)), ((), ())), preferred_element_type=jnp.float32
    )
    even = lax.rem(lax.broadcasted_iota(jnp.int32, (count, 1), 0), 2) == 0
    zero = jnp.zeros((count, 1), jnp.float32)
    slots = [zero] + [near[:, s : s + 1] for s in range(SLOTS)] + [zero]
    places = [jnp.where(even, slots[p], slots[p + 1]) for p in range(8)]
    low = lax.broadcasted_iota(jnp.int32, (count, 128), 1) < BLK
    for chunk in range(4):
        mask_ref[:, chunk * 128 : (chunk + 1) * 128] = jnp.where(
            low, places[2 * chunk], places[2 * chunk + 1]
        )


def pack_chip_kernel(l_ref, s_ref, h_ref, after_ref, *out_refs):
    del after_ref
    core = lax.rem(lax.axis_index("col"), 2)
    refs = {"l": l_ref, "s": s_ref, "h": h_ref}
    whole = {"l": 0, "s": 0, "h": 0}
    pl.when(core == 0)(lambda: write_halo(0, sender_block(refs, 0, whole), out_refs))
    pl.when(core == 1)(lambda: write_halo(1, sender_block(refs, 1, whole), out_refs))


def pack_chip(l_values, s_values, h_values, after):
    vmem = pl.BlockSpec(memory_space=pltpu.VMEM)
    return pl.pallas_call(
        pack_chip_kernel,
        out_shape=tuple(pltpu.VMEM((n, 128), jnp.bfloat16) for n in CHIP_PARTS),
        in_specs=[vmem] * 4,
        out_specs=(vmem,) * len(CHIP_PARTS),
        compiler_params=pltpu.CompilerParams(vmem_limit_bytes=8 * 1024 * 1024),
        cost_estimate=pl.CostEstimate(flops=1, bytes_accessed=1, transcendentals=0),
        name="pack_chip",
    )(l_values, s_values, h_values, after)


NAMES = ("s", "l", "h", "p", "t", "g")
RANGE = {"s": (-6, 16), "l": (-4, 13), "h": (-3, 13), "p": (-4, 13), "t": (-1, 9), "g": (-3, 13)}
FACTORS = {"p": ("l", "s"), "t": ("p", "l"), "g": ("h", "p"), "k": ("t", "p")}
GROUPS = {"p": range(-3, 13, 2), "t": range(-1, 9, 2), "g": range(-3, 13, 2), "k": range(-1, 9, 2)}
OFFSET = (-2, -1, -1, 0, 0, 1, 1, 2)
HALVES = ((0, 2), (2, 4))
PIECES = {
    ("p", -3): ((1, 2), (2, 4)),
    ("p", 9): ((0, 2), (2, 3)),
    ("p", 11): ((0, 2),),
    ("g", -3): ((3, 4),),
    ("g", 9): ((0, 2),),
    ("g", 11): ((0, 1),),
}
DEPTH = {("g", -3): (1, 4), ("g", 9): (0, 3), ("g", 11): (0, 2)}
SINGLE = {("t", -1): (1,), ("k", -1): (1,)}
HALO = (
    {"s": range(-6, 0), "l": range(-3, 0), "h": range(-3, 0)},
    {"s": range(9, 15), "l": range(9, 12), "h": range(9, 12)},
)
ZERO_ROWS = ((("l", -4), ("p", -4)), (("s", 15), ("l", 12), ("h", 12)))
ZERO_CHUNKS = (((-3, 0),), ((9, 3), (11, 2), (11, 3)))


@functools.cache
def phase_of(core, name, q):
    if name in ("s", "l", "h") or q < -3:
        if 0 <= q < ROWS:
            return 0
        return 2 if (q < 0) == (core == 0) else 1
    group = q if q % 2 else q - 1
    left, right = FACTORS[name]
    first, last = DEPTH.get((name, group), (0, 4))
    rows = range(group - REACH + 2 * first, group - REACH + 2 * last)
    return max(
        [phase_of(core, left, group + k) for k in (0, 1)]
        + [phase_of(core, right, m) for m in rows]
    )


@functools.cache
def early_pairs(core, name, q):
    left, right = FACTORS[name]
    if phase_of(core, name, q) < 2 or max(phase_of(core, left, q + k) for k in (0, 1)) == 2:
        return None
    first, last = DEPTH.get((name, q), (0, 4))
    pairs = [
        a
        for a in range(first, last)
        if max(phase_of(core, right, q - REACH + 2 * a + k) for k in (0, 1)) < 2
    ]
    if not pairs or (pairs[0] != first and pairs[-1] != last - 1):
        return None
    return pairs[0], pairs[-1] + 1


def partials_of(core, names):
    return [(name, q) for name in names for q in GROUPS[name] if early_pairs(core, name, q)]


def rows_of(name, q, count=1):
    first = (q - RANGE[name][0]) * BLK
    return slice(first, first + count * BLK)


class Stored:
    def __init__(self, core, arrays, mask_ref, partial_refs):
        self.core, self.arrays, self.mask_ref = core, arrays, mask_ref
        self.partial_refs = dict(zip(("p", "gk"), partial_refs))
        self.phase = len(arrays) - 1

    def get(self, name, q, first=0, last=4):
        ref = self.arrays[phase_of(self.core, name, q)][name]
        return ref[rows_of(name, q), first * 128 : last * 128]

    def put(self, name, q, values, first=0, last=4, count=1):
        ref = self.arrays[self.phase][name]
        ref[rows_of(name, q, count), first * 128 : last * 128] = values

    def mask(self, q, first, last):
        row = q - MASK_FIRST
        return self.mask_ref[row : row + 1, first * 128 : last * 128].astype(jnp.bfloat16)

    def pair_mask(self, name, q, first, last):
        shape = (BLK, (last - first) * 128)
        return jnp.concatenate(
            [
                jnp.broadcast_to(self.mask(q + k, first, last), shape)
                for k in SINGLE.get((name, q), (0, 1))
            ],
            axis=0,
        )

    def own_rows(self, refs):
        pad = jnp.zeros((BLK, BLK), jnp.bfloat16)
        for name, ref in refs.items():
            for q in range(ROWS):
                values = ref[q]
                parts = [pad, values] if shift_of(q) else [values, pad]
                stored = jnp.concatenate(parts, axis=1)
                self.put(name, q, stored * self.mask(q, 0, 4))

    def unpack(self, side, refs):
        pad = jnp.zeros((BLK, BLK), jnp.bfloat16)
        content = {}
        for n, keys in enumerate(PLANS[side]):
            for half, key in enumerate(keys):
                if key is not None:
                    content[key] = (n, half)

        def piece(n, first, last):
            place = n * BLK
            for ref in refs:
                if place < ref.shape[0]:
                    break
                place -= ref.shape[0]
            if n == CHUNKS - 1:
                halves = ref[place : place + BLK // 2, :]
                return jnp.concatenate([halves[:, :BLK], halves[:, BLK:]], axis=0)
            return ref[place : place + BLK, first * BLK : last * BLK]

        for name, rows in HALO[side].items():
            for q in rows:
                for chunk in range(4):
                    a, b = (content.get((name, q, 2 * chunk + half)) for half in (0, 1))
                    if a is None and b is None:
                        values = jnp.zeros((BLK, 128), jnp.bfloat16)
                    else:
                        if a is not None and b is not None and a[0] == b[0]:
                            values = piece(a[0], 0, 2)
                        else:
                            values = jnp.concatenate(
                                [pad if p is None else piece(p[0], p[1], p[1] + 1) for p in (a, b)],
                                axis=1,
                            )
                        values = values * self.mask(q, chunk, chunk + 1)
                    self.put(name, q, values, chunk, chunk + 1)
        for name, q in ZERO_ROWS[side]:
            self.put(name, q, jnp.zeros((BLK, LANES), jnp.bfloat16))
        for q, chunk in ZERO_CHUNKS[side]:
            zero = jnp.zeros((2 * BLK, 128), jnp.bfloat16)
            self.put("p", q, zero, chunk, chunk + 1, 2)

    def product(self, name, q, first, last, pairs):
        left, right = FACTORS[name]
        used = SINGLE.get((name, q), (0, 1))
        lhs = jnp.concatenate([self.get(left, q + k, *pairs) for k in used], axis=0)
        slabs = []
        for r in range(2 * pairs[0], 2 * pairs[1]):
            parts = []
            for chunk in range(first, last):
                source = chunk - OFFSET[r]
                if 0 <= source < 4:
                    parts.append(self.get(right, q - REACH + r, source, source + 1))
                else:
                    parts.append(jnp.zeros((BLK, 128), jnp.bfloat16))
            slabs.append(jnp.concatenate(parts, axis=1))
        rhs = jnp.concatenate(slabs, axis=0)
        return jnp.dot(lhs, rhs, preferred_element_type=jnp.float32)

    def partial_at(self, name, q):
        names = "p" if name == "p" else "gk"
        place = partials_of(self.core, names).index((name, q)) * 2 * BLK
        return self.partial_refs[names], slice(place, place + 2 * BLK)

    def put_partials(self, names):
        for name, q in partials_of(self.core, names):
            ref, rows = self.partial_at(name, q)
            for first, last in PIECES.get((name, q), HALVES):
                values = self.product(name, q, first, last, early_pairs(self.core, name, q))
                ref[rows, first * 128 : last * 128] = values

    def group(self, name, q):
        pairs, early = DEPTH.get((name, q), (0, 4)), None
        if self.phase == 2:
            early = early_pairs(self.core, name, q)
        if early:
            pairs = (early[1], pairs[1]) if early[0] == pairs[0] else (pairs[0], early[0])
        for first, last in PIECES.get((name, q), HALVES):
            values = self.product(name, q, first, last, pairs)
            if early:
                ref, rows = self.partial_at(name, q)
                values += ref[rows, first * 128 : last * 128]
            yield first, last, values

    def put_group(self, name, q):
        for first, last, values in self.group(name, q):
            values = values.astype(jnp.bfloat16) * self.pair_mask(name, q, first, last)
            used = SINGLE.get((name, q), (0, 1))
            self.put(name, q + used[0], values, first, last, len(used))

    def put_groups(self, names):
        for name in names:
            for q in GROUPS[name]:
                if phase_of(self.core, name, q) == self.phase:
                    self.put_group(name, q)

    def kernel_rows(self, q, out_ref):
        values = []
        used = SINGLE.get(("k", q), (0, 1))
        for first, last, quintic in self.group("k", q):
            lsl = jnp.concatenate([self.get("t", q + k, first, last) for k in used], axis=0)
            halved = (quintic - 1.5 * lsl.astype(jnp.float32)).astype(jnp.bfloat16)
            values.append(halved * (-2.0 * self.pair_mask("k", q, first, last)))
        values = jnp.concatenate(values, axis=1)
        if len(used) == 2:
            out_ref[q] = values[:BLK, : SLOTS * BLK]
        out_ref[q + 1] = values[-BLK:, BLK:]

    def gradient_rows(self, pair, out_ref):
        rows = [2 * pair + k for k in (0, 1) if 2 * pair + k < ROWS]
        zero = jnp.zeros((BLK, 128), jnp.bfloat16)
        mirrored = {}
        for step in range(-2, 3 if len(rows) == 2 else 2):
            upper = lower = zero
            if step >= -1:
                upper = self.get("g", 2 * (pair + step), 2 - step, 3 - step)
            if step <= 1:
                lower = self.get("g", 2 * (pair + step) + 1, 1 - step, 2 - step)
            mirrored[step] = jnp.transpose(jnp.concatenate([upper, lower], axis=0))
        for k, q in enumerate(rows):
            chunks = []
            for chunk in range(4):
                other = mirrored[chunk - 2 + k][k * BLK : (k + 1) * BLK]
                own = self.get("g", q, chunk, chunk + 1)
                chunks.append((own + other) * self.mask(q, chunk, chunk + 1))
            values = jnp.concatenate(chunks, axis=1)
            out_ref[q] = values[:, : SLOTS * BLK] if k else values[:, BLK:]


def stored_types(names):
    return tuple(
        pltpu.VMEM(((RANGE[name][1] - RANGE[name][0]) * BLK, LANES), jnp.bfloat16)
        for name in names
    )


def on_core(run):
    core = lax.rem(lax.axis_index("col"), 2)
    pl.when(core == 0)(lambda: run(0))
    pl.when(core == 1)(lambda: run(1))


LATE_ROUNDS = (
    (
        ("p1", "p-1", "p-3", "g5", "g3", "G4", "t1", "g1", "G3", "t-1",),
        ("g-1", "G2", "k5",),
        ("g-3", "G1", "k3",),
        ("k1", "G0",),
        ("k-1",),
    ),
    (
        ("p5", "p7", "p9", "p11", "g1", "g3", "g5", "G0", "t5", "t7", "g7", "G1",),
        ("g9", "k1", "G2",),
        ("g11", "k3", "G3",),
        ("k5", "G4",),
        ("k7",),
    ),
)
OWN_NAMES = ("s", "l", "h", "p", "t")
ROWS_TYPE = pltpu.VMEM((ROWS, BLK, SLOTS * BLK), jnp.bfloat16)


def vmem_call(kernel, operands, out_shape, name):
    vmem = pl.BlockSpec(memory_space=pltpu.VMEM)
    return pl.pallas_call(
        kernel,
        out_shape=out_shape,
        in_specs=[vmem] * len(operands),
        out_specs=(vmem,) * len(out_shape),
        compiler_params=pltpu.CompilerParams(vmem_limit_bytes=8 * 1024 * 1024),
        cost_estimate=pl.CostEstimate(flops=1, bytes_accessed=1, transcendentals=0),
        name=name,
    )(*operands)


def partial_type(names):
    count = max(len(partials_of(core, names)) for core in (0, 1))
    return pltpu.VMEM((count * 2 * BLK, LANES), jnp.float32)


def own_kernel(l_ref, s_ref, h_ref, pattern_ref, *outs):
    *outs, partial_ref, mask_ref = outs
    write_mask(pattern_ref, mask_ref)

    def run(core):
        st = Stored(core, [dict(zip(OWN_NAMES, outs))], mask_ref, [partial_ref])
        st.own_rows({"s": s_ref, "l": l_ref, "h": h_ref})
        st.put_groups("pt")
        st.put_partials("p")

    on_core(run)


def compute_own(l_values, s_values, h_values, turned):
    operands = (l_values, s_values, h_values, turned)
    mask = pltpu.VMEM((MASK_ROWS, LANES), jnp.float32)
    out = (*stored_types(OWN_NAMES), partial_type("p"), mask)
    *own, mask = vmem_call(own_kernel, operands, out, "own")
    return own, mask


def early_kernel(chip_a_ref, chip_b_ref, mask_ref, *refs):
    own, own_partial_ref = dict(zip(OWN_NAMES, refs[:5])), refs[5]
    early = dict(zip(NAMES, refs[6:12]))
    partial_ref, kernel_buf = refs[12:]

    def run(core):
        st = Stored(core, [own, early], mask_ref, [own_partial_ref, partial_ref])
        st.unpack(1 - core, (chip_a_ref, chip_b_ref))
        st.put_groups("ptg")
        for q in GROUPS["k"]:
            if phase_of(core, "k", q) < 2:
                st.kernel_rows(q, kernel_buf)
        st.put_partials("gk")

    on_core(run)


def compute_early(chip, mask, own):
    out = (*stored_types(NAMES), partial_type("gk"), ROWS_TYPE)
    return vmem_call(early_kernel, (*chip, mask, *own), out, "early")


def late_kernel(cross_ref, mask_ref, *refs):
    own, own_partial_ref = dict(zip(OWN_NAMES, refs[:5])), refs[5]
    early = dict(zip(NAMES, refs[6:12]))
    partial_ref, early_buf, kernel_hbm, gradient_hbm = refs[12:16]
    late = dict(zip(NAMES, refs[16:22]))
    kernel_buf, gradient_buf, sems = refs[22:]

    def run(core):
        st = Stored(core, [own, early, late], mask_ref, [own_partial_ref, partial_ref])
        copies = []

        def send(buf, hbm, first, last):
            for row in range(first, last):
                copy = pltpu.make_async_copy(buf.at[row], hbm.at[row], sems.at[len(copies)])
                copy.start()
                copies.append(copy)

        for q in GROUPS["k"]:
            if phase_of(core, "k", q) < 2:
                send(early_buf, kernel_hbm, max(q, 0), q + 2)
        st.unpack(core, (cross_ref,))
        for steps in LATE_ROUNDS[core]:
            ready = []
            for step in steps:
                name, q = step[0], int(step[1:])
                if name == "G":
                    st.gradient_rows(q, gradient_buf)
                    ready.append((gradient_buf, gradient_hbm, 2 * q, min(2 * q + 2, ROWS)))
                elif name == "k":
                    st.kernel_rows(q, kernel_buf)
                    ready.append((kernel_buf, kernel_hbm, max(q, 0), q + 2))
                else:
                    st.put_group(name, q)
            for item in ready:
                send(*item)
        for copy in copies:
            copy.wait()

    on_core(run)


def compute_late(cross, mask, own, early):
    vmem = pl.BlockSpec(memory_space=pltpu.VMEM)
    hbm = pl.BlockSpec(memory_space=pl.ANY)
    out = jax.ShapeDtypeStruct((ROWS, BLK, SLOTS * BLK), jnp.bfloat16)
    operands = (cross, mask, *own, *early)
    return pl.pallas_call(
        late_kernel,
        out_shape=(out, out),
        in_specs=[vmem] * len(operands),
        out_specs=(hbm, hbm),
        scratch_shapes=[
            *stored_types(NAMES),
            ROWS_TYPE,
            ROWS_TYPE,
            pltpu.SemaphoreType.DMA((2 * ROWS,)),
        ],
        compiler_params=pltpu.CompilerParams(vmem_limit_bytes=16 * 1024 * 1024),
        name="late",
    )(*operands)


def shards(l_values, s_values, h_values, pattern):
    count = lax.axis_size(AXES)
    cross_pairs, chip_pairs = [], []
    for i in range(0, count, 2):
        j = (i - 1) % count
        cross_pairs += [(i, j), (j, i)]
        chip_pairs += [(i, i + 1), (i + 1, i)]
    cross_out = pack_cross(l_values, s_values, h_values)
    cross = lax.ppermute(cross_out, AXES, cross_pairs)
    chip_out = pack_chip(l_values, s_values, h_values, cross_out)
    chip = [lax.ppermute(part, AXES, chip_pairs) for part in chip_out]
    own, mask = compute_own(l_values, s_values, h_values, pattern.T)
    early = compute_early(chip, mask, own)
    return compute_late(cross, mask, own, early)


def solution(mesh):
    rows = P(AXES, None, None)
    return jax.shard_map(
        shards,
        mesh=mesh,
        in_specs=(rows, rows, rows, P()),
        out_specs=(rows, rows),
        check_vma=False,
    )
```

```python
import functools

import jax
import jax.numpy as jnp
from jax import lax
from jax.experimental import pallas as pl
from jax.experimental.pallas import tpu as pltpu
from jax.sharding import PartitionSpec as P

BLK = 64
SLOTS = 7
REACH = 3
ROWS = 9
LANES = 512
AXES = ("dom", "col")


def shift_of(q):
    return 1 - q % 2


def column_of(q, position):
    return q - REACH + position - shift_of(q)


def halo_plan(side):
    if side == 0:
        rows = {"l": range(-3, 0), "s": range(-6, 0), "h": range(-3, 0)}
    else:
        rows = {"l": range(9, 12), "s": range(9, 15), "h": range(9, 12)}
    full, low, high = [], [], []
    for name in ("s", "l", "h"):
        for q in rows[name]:
            for chunk in range(4):
                need = []
                for position in (2 * chunk, 2 * chunk + 1):
                    slot = position - shift_of(q)
                    column = column_of(q, position)
                    inside = 0 <= slot < SLOTS
                    if name != "l":
                        inside = inside and (column >= -3 if side == 0 else column <= 11)
                    need.append(inside)
                a, b = (name, q, 2 * chunk), (name, q, 2 * chunk + 1)
                if all(need):
                    full.append((a, b))
                elif need[0]:
                    low.append(a)
                elif need[1]:
                    high.append(b)
    while low and high:
        full.append((low.pop(), high.pop()))
    rest = low + high
    while rest:
        a = rest.pop()
        full.append((a, rest.pop() if rest else None))
    return full


PLANS = (halo_plan(0), halo_plan(1))
CHUNKS = len(PLANS[0])
PACKED = CHUNKS * BLK - BLK // 2
CHIP_PARTS = (CHUNKS // 2 * BLK, PACKED - CHUNKS // 2 * BLK)
MASK_FIRST, MASK_ROWS = -6, 22


def write_halo(side, block, out_refs):
    for n, (a, b) in enumerate(PLANS[side]):
        ref, row, lane = block(*a)
        if b is None:
            only = ref[row, :, lane : lane + BLK]
            chunk = jnp.concatenate([only[: BLK // 2], only[BLK // 2 :]], axis=1)
        elif a[:2] == b[:2] and b[2] == a[2] + 1:
            chunk = ref[row, :, lane : lane + 2 * BLK]
        else:
            first = ref[row, :, lane : lane + BLK]
            ref, row, lane = block(*b)
            second = ref[row, :, lane : lane + BLK]
            chunk = jnp.concatenate([first, second], axis=1)
        place = n * BLK
        for out_ref in out_refs:
            if place < out_ref.shape[0]:
                break
            place -= out_ref.shape[0]
        out_ref[place : place + chunk.shape[0], :] = chunk


def sender_block(refs, side, first):
    def block(name, q, position):
        row = q - ROWS if side == 1 else q + ROWS
        return refs[name], row - first[name], (position - shift_of(q)) * BLK

    return block


def pack_cross_kernel(l_hbm, s_hbm, h_hbm, out_ref, l_buf, s_buf, h_buf, sems):
    core = lax.rem(lax.axis_index("col"), 2)
    copies = [
        pltpu.make_async_copy(s_hbm.at[pl.ds(3 * core, 6)], s_buf, sems.at[0]),
        pltpu.make_async_copy(l_hbm.at[pl.ds(6 * core, 3)], l_buf, sems.at[1]),
        pltpu.make_async_copy(h_hbm.at[pl.ds(6 * core, 3)], h_buf, sems.at[2]),
    ]
    for copy in copies:
        copy.start()
    bufs = {"l": l_buf, "s": s_buf, "h": h_buf}
    last = sender_block(bufs, 0, {"l": 6, "s": 3, "h": 6})
    first = sender_block(bufs, 1, {"l": 0, "s": 0, "h": 0})
    for copy in copies:
        copy.wait()
    pl.when(core == 1)(lambda: write_halo(0, last, (out_ref,)))
    pl.when(core == 0)(lambda: write_halo(1, first, (out_ref,)))


def pack_cross(l_values, s_values, h_values):
    hbm = pl.BlockSpec(memory_space=pltpu.HBM)
    return pl.pallas_call(
        pack_cross_kernel,
        out_shape=pltpu.VMEM((PACKED, 128), jnp.bfloat16),
        in_specs=[hbm] * 3,
        out_specs=pl.BlockSpec(memory_space=pltpu.VMEM),
        scratch_shapes=[
            pltpu.VMEM((3, BLK, SLOTS * BLK), jnp.bfloat16),
            pltpu.VMEM((6, BLK, SLOTS * BLK), jnp.bfloat16),
            pltpu.VMEM((3, BLK, SLOTS * BLK), jnp.bfloat16),
            pltpu.SemaphoreType.DMA((3,)),
        ],
        cost_estimate=pl.CostEstimate(flops=1, bytes_accessed=1, transcendentals=0),
        name="pack_cross",
    )(l_values, s_values, h_values)


def write_mask(pattern_ref, mask_ref):
    count, total = mask_ref.shape[0], pattern_ref.shape[1]
    device = lax.axis_index("dom") * lax.axis_size("col") + lax.axis_index("col")
    first = device * ROWS + MASK_FIRST + total
    wanted = lax.rem(first + lax.broadcasted_iota(jnp.int32, (count, total), 0), total)
    index = lax.broadcasted_iota(jnp.int32, (count, total), 1)
    picked = (wanted == index).astype(jnp.float32).astype(jnp.bfloat16)
    pattern = pattern_ref[...].astype(jnp.float32).astype(jnp.bfloat16)
    near = lax.dot_general(
        picked, pattern, (((1,), (1,)), ((), ())), preferred_element_type=jnp.float32
    )
    even = lax.rem(lax.broadcasted_iota(jnp.int32, (count, 1), 0), 2) == 0
    zero = jnp.zeros((count, 1), jnp.float32)
    slots = [zero] + [near[:, s : s + 1] for s in range(SLOTS)] + [zero]
    places = [jnp.where(even, slots[p], slots[p + 1]) for p in range(8)]
    low = lax.broadcasted_iota(jnp.int32, (count, 128), 1) < BLK
    for chunk in range(4):
        mask_ref[:, chunk * 128 : (chunk + 1) * 128] = jnp.where(
            low, places[2 * chunk], places[2 * chunk + 1]
        )


def pack_chip_kernel(l_ref, s_ref, h_ref, after_ref, *out_refs):
    del after_ref
    core = lax.rem(lax.axis_index("col"), 2)
    refs = {"l": l_ref, "s": s_ref, "h": h_ref}
    whole = {"l": 0, "s": 0, "h": 0}
    pl.when(core == 0)(lambda: write_halo(0, sender_block(refs, 0, whole), out_refs))
    pl.when(core == 1)(lambda: write_halo(1, sender_block(refs, 1, whole), out_refs))


def pack_chip(l_values, s_values, h_values, after):
    vmem = pl.BlockSpec(memory_space=pltpu.VMEM)
    return pl.pallas_call(
        pack_chip_kernel,
        out_shape=tuple(pltpu.VMEM((n, 128), jnp.bfloat16) for n in CHIP_PARTS),
        in_specs=[vmem] * 4,
        out_specs=(vmem,) * len(CHIP_PARTS),
        compiler_params=pltpu.CompilerParams(vmem_limit_bytes=8 * 1024 * 1024),
        cost_estimate=pl.CostEstimate(flops=1, bytes_accessed=1, transcendentals=0),
        name="pack_chip",
    )(l_values, s_values, h_values, after)


NAMES = ("s", "l", "h", "p", "t", "g")
RANGE = {"s": (-6, 16), "l": (-4, 13), "h": (-3, 13), "p": (-4, 13), "t": (-1, 9), "g": (-3, 13)}
FACTORS = {"p": ("l", "s"), "t": ("p", "l"), "g": ("h", "p"), "k": ("t", "p")}
GROUPS = {"p": range(-3, 13, 2), "t": range(-1, 9, 2), "g": range(-3, 13, 2), "k": range(-1, 9, 2)}
OFFSET = (-2, -1, -1, 0, 0, 1, 1, 2)
HALVES = ((0, 2), (2, 4))
PIECES = {
    ("p", -3): ((1, 2), (2, 4)),
    ("p", 9): ((0, 2), (2, 3)),
    ("p", 11): ((0, 2),),
    ("g", -3): ((3, 4),),
    ("g", 9): ((0, 2),),
    ("g", 11): ((0, 1),),
}
DEPTH = {("g", -3): (1, 4), ("g", 9): (0, 3), ("g", 11): (0, 2)}
SINGLE = {("t", -1): (1,), ("k", -1): (1,)}
HALO = (
    {"s": range(-6, 0), "l": range(-3, 0), "h": range(-3, 0)},
    {"s": range(9, 15), "l": range(9, 12), "h": range(9, 12)},
)
ZERO_ROWS = ((("l", -4), ("p", -4)), (("s", 15), ("l", 12), ("h", 12)))
ZERO_CHUNKS = (((-3, 0),), ((9, 3), (11, 2), (11, 3)))


@functools.cache
def phase_of(core, name, q):
    if name in ("s", "l", "h") or q < -3:
        if 0 <= q < ROWS:
            return 0
        return 2 if (q < 0) == (core == 0) else 1
    group = q if q % 2 else q - 1
    left, right = FACTORS[name]
    first, last = DEPTH.get((name, group), (0, 4))
    rows = range(group - REACH + 2 * first, group - REACH + 2 * last)
    return max(
        [phase_of(core, left, group + k) for k in (0, 1)]
        + [phase_of(core, right, m) for m in rows]
    )


@functools.cache
def early_pairs(core, name, q):
    left, right = FACTORS[name]
    if name == "g" and q in GROUPS["k"] and early_pairs(core, "k", q) is None:
        return None
    if phase_of(core, name, q) < 2 or max(phase_of(core, left, q + k) for k in (0, 1)) == 2:
        return None
    first, last = DEPTH.get((name, q), (0, 4))
    pairs = [
        a
        for a in range(first, last)
        if max(phase_of(core, right, q - REACH + 2 * a + k) for k in (0, 1)) < 2
    ]
    if not pairs or (pairs[0] != first and pairs[-1] != last - 1):
        return None
    return pairs[0], pairs[-1] + 1


def partials_of(core, names):
    return [(name, q) for name in names for q in GROUPS[name] if early_pairs(core, name, q)]


def rows_of(name, q, count=1):
    first = (q - RANGE[name][0]) * BLK
    return slice(first, first + count * BLK)


class Stored:
    def __init__(self, core, arrays, mask_ref, partial_refs):
        self.core, self.arrays, self.mask_ref = core, arrays, mask_ref
        self.partial_refs = dict(zip(("p", "gk"), partial_refs))
        self.phase = len(arrays) - 1

    def get(self, name, q, first=0, last=4):
        ref = self.arrays[phase_of(self.core, name, q)][name]
        return ref[rows_of(name, q), first * 128 : last * 128]

    def put(self, name, q, values, first=0, last=4, count=1):
        ref = self.arrays[self.phase][name]
        ref[rows_of(name, q, count), first * 128 : last * 128] = values

    def mask(self, q, first, last):
        row = q - MASK_FIRST
        return self.mask_ref[row : row + 1, first * 128 : last * 128].astype(jnp.bfloat16)

    def pair_mask(self, name, q, first, last):
        shape = (BLK, (last - first) * 128)
        return jnp.concatenate(
            [
                jnp.broadcast_to(self.mask(q + k, first, last), shape)
                for k in SINGLE.get((name, q), (0, 1))
            ],
            axis=0,
        )

    def own_rows(self, refs):
        pad = jnp.zeros((BLK, BLK), jnp.bfloat16)
        for name, ref in refs.items():
            for q in range(ROWS):
                values = ref[q]
                parts = [pad, values] if shift_of(q) else [values, pad]
                stored = jnp.concatenate(parts, axis=1)
                self.put(name, q, stored * self.mask(q, 0, 4))

    def unpack(self, side, refs):
        pad = jnp.zeros((BLK, BLK), jnp.bfloat16)
        content = {}
        for n, keys in enumerate(PLANS[side]):
            for half, key in enumerate(keys):
                if key is not None:
                    content[key] = (n, half)

        def piece(n, first, last):
            place = n * BLK
            for ref in refs:
                if place < ref.shape[0]:
                    break
                place -= ref.shape[0]
            if n == CHUNKS - 1:
                halves = ref[place : place + BLK // 2, :]
                return jnp.concatenate([halves[:, :BLK], halves[:, BLK:]], axis=0)
            return ref[place : place + BLK, first * BLK : last * BLK]

        for name, rows in HALO[side].items():
            for q in rows:
                for chunk in range(4):
                    a, b = (content.get((name, q, 2 * chunk + half)) for half in (0, 1))
                    if a is None and b is None:
                        values = jnp.zeros((BLK, 128), jnp.bfloat16)
                    else:
                        if a is not None and b is not None and a[0] == b[0]:
                            values = piece(a[0], 0, 2)
                        else:
                            values = jnp.concatenate(
                                [pad if p is None else piece(p[0], p[1], p[1] + 1) for p in (a, b)],
                                axis=1,
                            )
                        values = values * self.mask(q, chunk, chunk + 1)
                    self.put(name, q, values, chunk, chunk + 1)
        for name, q in ZERO_ROWS[side]:
            self.put(name, q, jnp.zeros((BLK, LANES), jnp.bfloat16))
        for q, chunk in ZERO_CHUNKS[side]:
            zero = jnp.zeros((2 * BLK, 128), jnp.bfloat16)
            self.put("p", q, zero, chunk, chunk + 1, 2)

    def multiply(self, factors, right, q, first, last, pairs):
        lhs = jnp.concatenate([self.get(name, row, *pairs) for name, row in factors], axis=0)
        slabs = []
        for r in range(2 * pairs[0], 2 * pairs[1]):
            parts = []
            for chunk in range(first, last):
                source = chunk - OFFSET[r]
                if 0 <= source < 4:
                    parts.append(self.get(right, q - REACH + r, source, source + 1))
                else:
                    parts.append(jnp.zeros((BLK, 128), jnp.bfloat16))
            slabs.append(jnp.concatenate(parts, axis=1))
        rhs = jnp.concatenate(slabs, axis=0)
        return jnp.dot(lhs, rhs, preferred_element_type=jnp.float32)

    def factors_of(self, name, q):
        return [(FACTORS[name][0], q + k) for k in SINGLE.get((name, q), (0, 1))]

    def product(self, name, q, first, last, pairs):
        right = FACTORS[name][1]
        return self.multiply(self.factors_of(name, q), right, q, first, last, pairs)

    def partial_at(self, name, q):
        names = "p" if name == "p" else "gk"
        place = partials_of(self.core, names).index((name, q)) * 2 * BLK
        return self.partial_refs[names], slice(place, place + 2 * BLK)

    def put_partials(self, names):
        for name, q in partials_of(self.core, names):
            ref, rows = self.partial_at(name, q)
            for first, last in PIECES.get((name, q), HALVES):
                values = self.product(name, q, first, last, early_pairs(self.core, name, q))
                ref[rows, first * 128 : last * 128] = values

    def late_pairs(self, name, q):
        pairs, early = DEPTH.get((name, q), (0, 4)), None
        if self.phase == 2:
            early = early_pairs(self.core, name, q)
        if early:
            pairs = (early[1], pairs[1]) if early[0] == pairs[0] else (pairs[0], early[0])
        return pairs, early is not None

    def add_partial(self, name, q, first, last, values):
        ref, rows = self.partial_at(name, q)
        return values + ref[rows, first * 128 : last * 128]

    def group(self, name, q):
        pairs, partial = self.late_pairs(name, q)
        for first, last in PIECES.get((name, q), HALVES):
            values = self.product(name, q, first, last, pairs)
            if partial:
                values = self.add_partial(name, q, first, last, values)
            yield first, last, values

    def put_piece(self, name, q, first, last, values):
        values = values.astype(jnp.bfloat16) * self.pair_mask(name, q, first, last)
        used = SINGLE.get((name, q), (0, 1))
        self.put(name, q + used[0], values, first, last, len(used))

    def put_group(self, name, q):
        for first, last, values in self.group(name, q):
            self.put_piece(name, q, first, last, values)

    def put_both(self, q, out_ref):
        pairs, partial = self.late_pairs("g", q)
        assert self.late_pairs("k", q) == (pairs, partial)
        factors = self.factors_of("g", q) + self.factors_of("k", q)
        pieces = []
        for first, last in HALVES:
            values = self.multiply(factors, "p", q, first, last, pairs)
            hls, quintic = values[: 2 * BLK], values[2 * BLK :]
            if partial:
                hls = self.add_partial("g", q, first, last, hls)
                quintic = self.add_partial("k", q, first, last, quintic)
            self.put_piece("g", q, first, last, hls)
            pieces.append((first, last, quintic))
        self.kernel_rows(q, out_ref, pieces)

    def put_groups(self, names):
        for name in names:
            for q in GROUPS[name]:
                if phase_of(self.core, name, q) == self.phase:
                    self.put_group(name, q)

    def kernel_rows(self, q, out_ref, pieces):
        values = []
        used = SINGLE.get(("k", q), (0, 1))
        for first, last, quintic in pieces:
            lsl = jnp.concatenate([self.get("t", q + k, first, last) for k in used], axis=0)
            halved = (quintic - 1.5 * lsl.astype(jnp.float32)).astype(jnp.bfloat16)
            values.append(halved * (-2.0 * self.pair_mask("k", q, first, last)))
        values = jnp.concatenate(values, axis=1)
        if len(used) == 2:
            out_ref[q] = values[:BLK, : SLOTS * BLK]
        out_ref[q + 1] = values[-BLK:, BLK:]

    def gradient_rows(self, pair, out_ref):
        rows = [2 * pair + k for k in (0, 1) if 2 * pair + k < ROWS]
        zero = jnp.zeros((BLK, 128), jnp.bfloat16)
        mirrored = {}
        for step in range(-2, 3 if len(rows) == 2 else 2):
            upper = lower = zero
            if step >= -1:
                upper = self.get("g", 2 * (pair + step), 2 - step, 3 - step)
            if step <= 1:
                lower = self.get("g", 2 * (pair + step) + 1, 1 - step, 2 - step)
            mirrored[step] = jnp.transpose(jnp.concatenate([upper, lower], axis=0))
        for k, q in enumerate(rows):
            chunks = []
            for chunk in range(4):
                other = mirrored[chunk - 2 + k][k * BLK : (k + 1) * BLK]
                own = self.get("g", q, chunk, chunk + 1)
                chunks.append((own + other) * self.mask(q, chunk, chunk + 1))
            values = jnp.concatenate(chunks, axis=1)
            out_ref[q] = values[:, : SLOTS * BLK] if k else values[:, BLK:]


def stored_types(names):
    return tuple(
        pltpu.VMEM(((RANGE[name][1] - RANGE[name][0]) * BLK, LANES), jnp.bfloat16)
        for name in names
    )


def on_core(run):
    core = lax.rem(lax.axis_index("col"), 2)
    pl.when(core == 0)(lambda: run(0))
    pl.when(core == 1)(lambda: run(1))


LATE_ROUNDS = (
    (
        ("p1", "p-1", "p-3", "b5", "b3", "G4", "t1", "t-1", "G3",),
        ("b1", "G2",),
        ("b-1", "G1",),
        ("g-3", "G0",),
    ),
    (
        ("p5", "p7", "p9", "p11", "b1", "b3", "t5", "t7", "G0",),
        ("b5", "G1",),
        ("b7", "G2",),
        ("g9", "G3",),
        ("g11", "G4",),
    ),
)
OWN_NAMES = ("s", "l", "h", "p", "t")
ROWS_TYPE = pltpu.VMEM((ROWS, BLK, SLOTS * BLK), jnp.bfloat16)


def vmem_call(kernel, operands, out_shape, name):
    vmem = pl.BlockSpec(memory_space=pltpu.VMEM)
    return pl.pallas_call(
        kernel,
        out_shape=out_shape,
        in_specs=[vmem] * len(operands),
        out_specs=(vmem,) * len(out_shape),
        compiler_params=pltpu.CompilerParams(vmem_limit_bytes=8 * 1024 * 1024),
        cost_estimate=pl.CostEstimate(flops=1, bytes_accessed=1, transcendentals=0),
        name=name,
    )(*operands)


def partial_type(names):
    count = max(len(partials_of(core, names)) for core in (0, 1))
    return pltpu.VMEM((count * 2 * BLK, LANES), jnp.float32)


def own_kernel(l_ref, s_ref, h_ref, pattern_ref, *outs):
    *outs, partial_ref, mask_ref = outs
    write_mask(pattern_ref, mask_ref)

    def run(core):
        st = Stored(core, [dict(zip(OWN_NAMES, outs))], mask_ref, [partial_ref])
        st.own_rows({"s": s_ref, "l": l_ref, "h": h_ref})
        st.put_groups("pt")
        st.put_partials("p")

    on_core(run)


def compute_own(l_values, s_values, h_values, turned):
    operands = (l_values, s_values, h_values, turned)
    mask = pltpu.VMEM((MASK_ROWS, LANES), jnp.float32)
    out = (*stored_types(OWN_NAMES), partial_type("p"), mask)
    *own, mask = vmem_call(own_kernel, operands, out, "own")
    return own, mask


def early_kernel(chip_a_ref, chip_b_ref, mask_ref, *refs):
    own, own_partial_ref = dict(zip(OWN_NAMES, refs[:5])), refs[5]
    early = dict(zip(NAMES, refs[6:12]))
    partial_ref, kernel_buf = refs[12:]

    def run(core):
        st = Stored(core, [own, early], mask_ref, [own_partial_ref, partial_ref])
        st.unpack(1 - core, (chip_a_ref, chip_b_ref))
        st.put_groups("ptg")
        for q in GROUPS["k"]:
            if phase_of(core, "k", q) < 2:
                st.kernel_rows(q, kernel_buf, st.group("k", q))
        st.put_partials("gk")

    on_core(run)


def compute_early(chip, mask, own):
    out = (*stored_types(NAMES), partial_type("gk"), ROWS_TYPE)
    return vmem_call(early_kernel, (*chip, mask, *own), out, "early")


def late_kernel(cross_ref, mask_ref, *refs):
    own, own_partial_ref = dict(zip(OWN_NAMES, refs[:5])), refs[5]
    early = dict(zip(NAMES, refs[6:12]))
    partial_ref, early_buf, kernel_hbm, gradient_hbm = refs[12:16]
    late = dict(zip(NAMES, refs[16:22]))
    kernel_buf, gradient_buf, sems = refs[22:]

    def run(core):
        st = Stored(core, [own, early, late], mask_ref, [own_partial_ref, partial_ref])
        copies = []

        def send(buf, hbm, first, last):
            for row in range(first, last):
                copy = pltpu.make_async_copy(buf.at[row], hbm.at[row], sems.at[len(copies)])
                copy.start()
                copies.append(copy)

        for q in GROUPS["k"]:
            if phase_of(core, "k", q) < 2:
                send(early_buf, kernel_hbm, max(q, 0), q + 2)
        st.unpack(core, (cross_ref,))
        for steps in LATE_ROUNDS[core]:
            ready = []
            for step in steps:
                name, q = step[0], int(step[1:])
                if name == "G":
                    st.gradient_rows(q, gradient_buf)
                    ready.append((gradient_buf, gradient_hbm, 2 * q, min(2 * q + 2, ROWS)))
                elif name == "b":
                    st.put_both(q, kernel_buf)
                    ready.append((kernel_buf, kernel_hbm, max(q, 0), q + 2))
                else:
                    st.put_group(name, q)
            for item in ready:
                send(*item)
        for copy in copies:
            copy.wait()

    on_core(run)


def compute_late(cross, mask, own, early):
    vmem = pl.BlockSpec(memory_space=pltpu.VMEM)
    hbm = pl.BlockSpec(memory_space=pl.ANY)
    out = jax.ShapeDtypeStruct((ROWS, BLK, SLOTS * BLK), jnp.bfloat16)
    operands = (cross, mask, *own, *early)
    return pl.pallas_call(
        late_kernel,
        out_shape=(out, out),
        in_specs=[vmem] * len(operands),
        out_specs=(hbm, hbm),
        scratch_shapes=[
            *stored_types(NAMES),
            ROWS_TYPE,
            ROWS_TYPE,
            pltpu.SemaphoreType.DMA((2 * ROWS,)),
        ],
        compiler_params=pltpu.CompilerParams(vmem_limit_bytes=16 * 1024 * 1024),
        name="late",
    )(*operands)


def shards(l_values, s_values, h_values, pattern):
    count = lax.axis_size(AXES)
    cross_pairs, chip_pairs = [], []
    for i in range(0, count, 2):
        j = (i - 1) % count
        cross_pairs += [(i, j), (j, i)]
        chip_pairs += [(i, i + 1), (i + 1, i)]
    cross_out = pack_cross(l_values, s_values, h_values)
    cross = lax.ppermute(cross_out, AXES, cross_pairs)
    chip_out = pack_chip(l_values, s_values, h_values, cross_out)
    chip = [lax.ppermute(part, AXES, chip_pairs) for part in chip_out]
    own, mask = compute_own(l_values, s_values, h_values, pattern.T)
    early = compute_early(chip, mask, own)
    return compute_late(cross, mask, own, early)


def solution(mesh):
    rows = P(AXES, None, None)
    return jax.shard_map(
        shards,
        mesh=mesh,
        in_specs=(rows, rows, rows, P()),
        out_specs=(rows, rows),
        check_vma=False,
    )
```

```python
import functools

import jax
import jax.numpy as jnp
from jax import lax
from jax.experimental import pallas as pl
from jax.experimental.pallas import tpu as pltpu
from jax.sharding import PartitionSpec as P

BLK = 64
SLOTS = 7
REACH = 3
ROWS = 9
LANES = 512
AXES = ("dom", "col")


def shift_of(q):
    return 1 - q % 2


def column_of(q, position):
    return q - REACH + position - shift_of(q)


def halo_plan(side):
    if side == 0:
        rows = {"l": range(-3, 0), "s": range(-6, 0), "h": range(-3, 0)}
    else:
        rows = {"l": range(9, 12), "s": range(9, 15), "h": range(9, 12)}
    full, low, high = [], [], []
    for name in ("s", "l", "h"):
        for q in rows[name]:
            for chunk in range(4):
                need = []
                for position in (2 * chunk, 2 * chunk + 1):
                    slot = position - shift_of(q)
                    column = column_of(q, position)
                    inside = 0 <= slot < SLOTS
                    if name != "l":
                        inside = inside and (column >= -3 if side == 0 else column <= 11)
                    need.append(inside)
                a, b = (name, q, 2 * chunk), (name, q, 2 * chunk + 1)
                if all(need):
                    full.append((a, b))
                elif need[0]:
                    low.append(a)
                elif need[1]:
                    high.append(b)
    while low and high:
        full.append((low.pop(), high.pop()))
    rest = low + high
    while rest:
        a = rest.pop()
        full.append((a, rest.pop() if rest else None))
    return full


PLANS = (halo_plan(0), halo_plan(1))
CHUNKS = len(PLANS[0])
PACKED = CHUNKS * BLK - BLK // 2
CHIP_PARTS = (CHUNKS // 2 * BLK, PACKED - CHUNKS // 2 * BLK)
MASK_FIRST, MASK_ROWS = -6, 22


def write_halo(side, block, out_refs):
    for n, (a, b) in enumerate(PLANS[side]):
        ref, row, lane = block(*a)
        if b is None:
            only = ref[row, :, lane : lane + BLK]
            chunk = jnp.concatenate([only[: BLK // 2], only[BLK // 2 :]], axis=1)
        elif a[:2] == b[:2] and b[2] == a[2] + 1:
            chunk = ref[row, :, lane : lane + 2 * BLK]
        else:
            first = ref[row, :, lane : lane + BLK]
            ref, row, lane = block(*b)
            second = ref[row, :, lane : lane + BLK]
            chunk = jnp.concatenate([first, second], axis=1)
        place = n * BLK
        for out_ref in out_refs:
            if place < out_ref.shape[0]:
                break
            place -= out_ref.shape[0]
        out_ref[place : place + chunk.shape[0], :] = chunk


def sender_block(refs, side, first):
    def block(name, q, position):
        row = q - ROWS if side == 1 else q + ROWS
        return refs[name], row - first[name], (position - shift_of(q)) * BLK

    return block


def pack_cross_kernel(l_hbm, s_hbm, h_hbm, out_ref, l_buf, s_buf, h_buf, sems):
    core = lax.rem(lax.axis_index("col"), 2)
    copies = [
        pltpu.make_async_copy(s_hbm.at[pl.ds(3 * core, 6)], s_buf, sems.at[0]),
        pltpu.make_async_copy(l_hbm.at[pl.ds(6 * core, 3)], l_buf, sems.at[1]),
        pltpu.make_async_copy(h_hbm.at[pl.ds(6 * core, 3)], h_buf, sems.at[2]),
    ]
    for copy in copies:
        copy.start()
    bufs = {"l": l_buf, "s": s_buf, "h": h_buf}
    last = sender_block(bufs, 0, {"l": 6, "s": 3, "h": 6})
    first = sender_block(bufs, 1, {"l": 0, "s": 0, "h": 0})
    for copy in copies:
        copy.wait()
    pl.when(core == 1)(lambda: write_halo(0, last, (out_ref,)))
    pl.when(core == 0)(lambda: write_halo(1, first, (out_ref,)))


def pack_cross(l_values, s_values, h_values):
    hbm = pl.BlockSpec(memory_space=pltpu.HBM)
    return pl.pallas_call(
        pack_cross_kernel,
        out_shape=pltpu.VMEM((PACKED, 128), jnp.bfloat16),
        in_specs=[hbm] * 3,
        out_specs=pl.BlockSpec(memory_space=pltpu.VMEM),
        scratch_shapes=[
            pltpu.VMEM((3, BLK, SLOTS * BLK), jnp.bfloat16),
            pltpu.VMEM((6, BLK, SLOTS * BLK), jnp.bfloat16),
            pltpu.VMEM((3, BLK, SLOTS * BLK), jnp.bfloat16),
            pltpu.SemaphoreType.DMA((3,)),
        ],
        cost_estimate=pl.CostEstimate(flops=1, bytes_accessed=1, transcendentals=0),
        name="pack_cross",
    )(l_values, s_values, h_values)


def write_mask(pattern_ref, mask_ref):
    count, total = mask_ref.shape[0], pattern_ref.shape[1]
    device = lax.axis_index("dom") * lax.axis_size("col") + lax.axis_index("col")
    first = device * ROWS + MASK_FIRST + total
    wanted = lax.rem(first + lax.broadcasted_iota(jnp.int32, (count, total), 0), total)
    index = lax.broadcasted_iota(jnp.int32, (count, total), 1)
    picked = (wanted == index).astype(jnp.float32).astype(jnp.bfloat16)
    pattern = pattern_ref[...].astype(jnp.float32).astype(jnp.bfloat16)
    near = lax.dot_general(
        picked, pattern, (((1,), (1,)), ((), ())), preferred_element_type=jnp.float32
    )
    even = lax.rem(lax.broadcasted_iota(jnp.int32, (count, 1), 0), 2) == 0
    zero = jnp.zeros((count, 1), jnp.float32)
    slots = [zero] + [near[:, s : s + 1] for s in range(SLOTS)] + [zero]
    places = [jnp.where(even, slots[p], slots[p + 1]) for p in range(8)]
    low = lax.broadcasted_iota(jnp.int32, (count, 128), 1) < BLK
    for chunk in range(4):
        mask_ref[:, chunk * 128 : (chunk + 1) * 128] = jnp.where(
            low, places[2 * chunk], places[2 * chunk + 1]
        )


def pack_chip_kernel(l_ref, s_ref, h_ref, after_ref, *out_refs):
    del after_ref
    core = lax.rem(lax.axis_index("col"), 2)
    refs = {"l": l_ref, "s": s_ref, "h": h_ref}
    whole = {"l": 0, "s": 0, "h": 0}
    pl.when(core == 0)(lambda: write_halo(0, sender_block(refs, 0, whole), out_refs))
    pl.when(core == 1)(lambda: write_halo(1, sender_block(refs, 1, whole), out_refs))


def pack_chip(l_values, s_values, h_values, after):
    vmem = pl.BlockSpec(memory_space=pltpu.VMEM)
    return pl.pallas_call(
        pack_chip_kernel,
        out_shape=tuple(pltpu.VMEM((n, 128), jnp.bfloat16) for n in CHIP_PARTS),
        in_specs=[vmem] * 4,
        out_specs=(vmem,) * len(CHIP_PARTS),
        compiler_params=pltpu.CompilerParams(vmem_limit_bytes=8 * 1024 * 1024),
        cost_estimate=pl.CostEstimate(flops=1, bytes_accessed=1, transcendentals=0),
        name="pack_chip",
    )(l_values, s_values, h_values, after)


NAMES = ("s", "l", "h", "p", "t", "g")
RANGE = {"s": (-6, 16), "l": (-4, 13), "h": (-3, 13), "p": (-4, 13), "t": (-1, 9), "g": (-3, 13)}
FACTORS = {"p": ("l", "s"), "t": ("p", "l"), "g": ("h", "p"), "k": ("t", "p")}
GROUPS = {"p": range(-3, 13, 2), "t": range(-1, 9, 2), "g": range(-3, 13, 2), "k": range(-1, 9, 2)}
OFFSET = (-2, -1, -1, 0, 0, 1, 1, 2)
HALVES = ((0, 2), (2, 4))
PIECES = {
    ("p", -3): ((1, 2), (2, 4)),
    ("p", 9): ((0, 2), (2, 3)),
    ("p", 11): ((0, 2),),
    ("g", -3): ((3, 4),),
    ("g", 9): ((0, 2),),
    ("g", 11): ((0, 1),),
}
DEPTH = {("g", -3): (1, 4), ("g", 9): (0, 3), ("g", 11): (0, 2)}
SINGLE = {("t", -1): (1,), ("k", -1): (1,)}
HALO = (
    {"s": range(-6, 0), "l": range(-3, 0), "h": range(-3, 0)},
    {"s": range(9, 15), "l": range(9, 12), "h": range(9, 12)},
)
ZERO_ROWS = ((("l", -4), ("p", -4)), (("s", 15), ("l", 12), ("h", 12)))
ZERO_CHUNKS = (((-3, 0),), ((9, 3), (11, 2), (11, 3)))


@functools.cache
def phase_of(core, name, q):
    if name in ("s", "l", "h") or q < -3:
        if 0 <= q < ROWS:
            return 0
        return 2 if (q < 0) == (core == 0) else 1
    group = q if q % 2 else q - 1
    left, right = FACTORS[name]
    first, last = DEPTH.get((name, group), (0, 4))
    rows = range(group - REACH + 2 * first, group - REACH + 2 * last)
    return max(
        [phase_of(core, left, group + k) for k in (0, 1)]
        + [phase_of(core, right, m) for m in rows]
    )


@functools.cache
def early_pairs(core, name, q):
    left, right = FACTORS[name]
    if name == "g" and q in GROUPS["k"] and early_pairs(core, "k", q) is None:
        return None
    if phase_of(core, name, q) < 2 or max(phase_of(core, left, q + k) for k in (0, 1)) == 2:
        return None
    first, last = DEPTH.get((name, q), (0, 4))
    pairs = [
        a
        for a in range(first, last)
        if max(phase_of(core, right, q - REACH + 2 * a + k) for k in (0, 1)) < 2
    ]
    if not pairs or (pairs[0] != first and pairs[-1] != last - 1):
        return None
    return pairs[0], pairs[-1] + 1


def partials_of(core, names):
    return [(name, q) for name in names for q in GROUPS[name] if early_pairs(core, name, q)]


def rows_of(name, q, count=1):
    first = (q - RANGE[name][0]) * BLK
    return slice(first, first + count * BLK)


class Stored:
    def __init__(self, core, arrays, mask_ref, partial_refs):
        self.core, self.arrays, self.mask_ref = core, arrays, mask_ref
        self.partial_refs = dict(zip(("p", "gk"), partial_refs))
        self.phase = len(arrays) - 1

    def get(self, name, q, first=0, last=4):
        ref = self.arrays[phase_of(self.core, name, q)][name]
        return ref[rows_of(name, q), first * 128 : last * 128]

    def put(self, name, q, values, first=0, last=4, count=1):
        ref = self.arrays[self.phase][name]
        ref[rows_of(name, q, count), first * 128 : last * 128] = values

    def mask(self, q, first, last):
        row = q - MASK_FIRST
        return self.mask_ref[row : row + 1, first * 128 : last * 128].astype(jnp.bfloat16)

    def pair_mask(self, name, q, first, last):
        shape = (BLK, (last - first) * 128)
        return jnp.concatenate(
            [
                jnp.broadcast_to(self.mask(q + k, first, last), shape)
                for k in SINGLE.get((name, q), (0, 1))
            ],
            axis=0,
        )

    def own_rows(self, refs):
        pad = jnp.zeros((BLK, BLK), jnp.bfloat16)
        for name, ref in refs.items():
            for q in range(ROWS):
                values = ref[q]
                parts = [pad, values] if shift_of(q) else [values, pad]
                stored = jnp.concatenate(parts, axis=1)
                self.put(name, q, stored * self.mask(q, 0, 4))

    def unpack(self, side, refs):
        pad = jnp.zeros((BLK, BLK), jnp.bfloat16)
        content = {}
        for n, keys in enumerate(PLANS[side]):
            for half, key in enumerate(keys):
                if key is not None:
                    content[key] = (n, half)

        def piece(n, first, last):
            place = n * BLK
            for ref in refs:
                if place < ref.shape[0]:
                    break
                place -= ref.shape[0]
            if n == CHUNKS - 1:
                halves = ref[place : place + BLK // 2, :]
                return jnp.concatenate([halves[:, :BLK], halves[:, BLK:]], axis=0)
            return ref[place : place + BLK, first * BLK : last * BLK]

        for name, rows in HALO[side].items():
            for q in rows:
                for chunk in range(4):
                    a, b = (content.get((name, q, 2 * chunk + half)) for half in (0, 1))
                    if a is None and b is None:
                        values = jnp.zeros((BLK, 128), jnp.bfloat16)
                    else:
                        if a is not None and b is not None and a[0] == b[0]:
                            values = piece(a[0], 0, 2)
                        else:
                            values = jnp.concatenate(
                                [pad if p is None else piece(p[0], p[1], p[1] + 1) for p in (a, b)],
                                axis=1,
                            )
                        values = values * self.mask(q, chunk, chunk + 1)
                    self.put(name, q, values, chunk, chunk + 1)
        for name, q in ZERO_ROWS[side]:
            self.put(name, q, jnp.zeros((BLK, LANES), jnp.bfloat16))
        for q, chunk in ZERO_CHUNKS[side]:
            zero = jnp.zeros((2 * BLK, 128), jnp.bfloat16)
            self.put("p", q, zero, chunk, chunk + 1, 2)

    def multiply(self, factors, right, q, first, last, pairs):
        lhs = jnp.concatenate([self.get(name, row, *pairs) for name, row in factors], axis=0)
        slabs = []
        for r in range(2 * pairs[0], 2 * pairs[1]):
            parts = []
            for chunk in range(first, last):
                source = chunk - OFFSET[r]
                if 0 <= source < 4:
                    parts.append(self.get(right, q - REACH + r, source, source + 1))
                else:
                    parts.append(jnp.zeros((BLK, 128), jnp.bfloat16))
            slabs.append(jnp.concatenate(parts, axis=1))
        rhs = jnp.concatenate(slabs, axis=0)
        return jnp.dot(lhs, rhs, preferred_element_type=jnp.float32)

    def factors_of(self, name, q):
        return [(FACTORS[name][0], q + k) for k in SINGLE.get((name, q), (0, 1))]

    def product(self, name, q, first, last, pairs):
        right = FACTORS[name][1]
        return self.multiply(self.factors_of(name, q), right, q, first, last, pairs)

    def partial_at(self, name, q):
        names = "p" if name == "p" else "gk"
        place = partials_of(self.core, names).index((name, q)) * 2 * BLK
        return self.partial_refs[names], slice(place, place + 2 * BLK)

    def put_partials(self, names):
        todo = partials_of(self.core, names)
        for name, q in todo:
            pairs = early_pairs(self.core, name, q)
            together = [name]
            if name == "k":
                continue
            if name == "g" and ("k", q) in todo:
                assert early_pairs(self.core, "k", q) == pairs
                together.append("k")
            factors = [factor for each in together for factor in self.factors_of(each, q)]
            for first, last in HALVES:
                values = self.multiply(factors, FACTORS[name][1], q, first, last, pairs)
                for n, each in enumerate(together):
                    ref, rows = self.partial_at(each, q)
                    part = values[n * 2 * BLK : (n + 1) * 2 * BLK]
                    ref[rows, first * 128 : last * 128] = part

    def late_pairs(self, name, q):
        pairs, early = DEPTH.get((name, q), (0, 4)), None
        if self.phase == 2:
            early = early_pairs(self.core, name, q)
        if early:
            pairs = (early[1], pairs[1]) if early[0] == pairs[0] else (pairs[0], early[0])
        return pairs, early is not None

    def add_partial(self, name, q, first, last, values):
        ref, rows = self.partial_at(name, q)
        return values + ref[rows, first * 128 : last * 128]

    def group(self, name, q):
        pairs, partial = self.late_pairs(name, q)
        for first, last in PIECES.get((name, q), HALVES):
            values = self.product(name, q, first, last, pairs)
            if partial:
                values = self.add_partial(name, q, first, last, values)
            yield first, last, values

    def put_piece(self, name, q, first, last, values):
        values = values.astype(jnp.bfloat16) * self.pair_mask(name, q, first, last)
        used = SINGLE.get((name, q), (0, 1))
        self.put(name, q + used[0], values, first, last, len(used))

    def put_group(self, name, q):
        for first, last, values in self.group(name, q):
            self.put_piece(name, q, first, last, values)

    def put_both(self, q, out_ref):
        pairs, partial = self.late_pairs("g", q)
        assert self.late_pairs("k", q) == (pairs, partial)
        factors = self.factors_of("g", q) + self.factors_of("k", q)
        pieces = []
        for first, last in HALVES:
            values = self.multiply(factors, "p", q, first, last, pairs)
            hls, quintic = values[: 2 * BLK], values[2 * BLK :]
            if partial:
                hls = self.add_partial("g", q, first, last, hls)
                quintic = self.add_partial("k", q, first, last, quintic)
            self.put_piece("g", q, first, last, hls)
            pieces.append((first, last, quintic))
        self.kernel_rows(q, out_ref, pieces)

    def put_groups(self, names):
        for name in names:
            for q in GROUPS[name]:
                if phase_of(self.core, name, q) == self.phase:
                    self.put_group(name, q)

    def kernel_rows(self, q, out_ref, pieces):
        values = []
        used = SINGLE.get(("k", q), (0, 1))
        for first, last, quintic in pieces:
            lsl = jnp.concatenate([self.get("t", q + k, first, last) for k in used], axis=0)
            halved = (quintic - 1.5 * lsl.astype(jnp.float32)).astype(jnp.bfloat16)
            values.append(halved * (-2.0 * self.pair_mask("k", q, first, last)))
        values = jnp.concatenate(values, axis=1)
        if len(used) == 2:
            out_ref[q] = values[:BLK, : SLOTS * BLK]
        out_ref[q + 1] = values[-BLK:, BLK:]

    def gradient_rows(self, pair, out_ref):
        rows = [2 * pair + k for k in (0, 1) if 2 * pair + k < ROWS]
        zero = jnp.zeros((BLK, 128), jnp.bfloat16)
        mirrored = {}
        for step in range(-2, 3 if len(rows) == 2 else 2):
            upper = lower = zero
            if step >= -1:
                upper = self.get("g", 2 * (pair + step), 2 - step, 3 - step)
            if step <= 1:
                lower = self.get("g", 2 * (pair + step) + 1, 1 - step, 2 - step)
            mirrored[step] = jnp.transpose(jnp.concatenate([upper, lower], axis=0))
        for k, q in enumerate(rows):
            chunks = []
            for chunk in range(4):
                other = mirrored[chunk - 2 + k][k * BLK : (k + 1) * BLK]
                own = self.get("g", q, chunk, chunk + 1)
                chunks.append((own + other) * self.mask(q, chunk, chunk + 1))
            values = jnp.concatenate(chunks, axis=1)
            out_ref[q] = values[:, : SLOTS * BLK] if k else values[:, BLK:]


def stored_types(names):
    return tuple(
        pltpu.VMEM(((RANGE[name][1] - RANGE[name][0]) * BLK, LANES), jnp.bfloat16)
        for name in names
    )


def on_core(run):
    core = lax.rem(lax.axis_index("col"), 2)
    pl.when(core == 0)(lambda: run(0))
    pl.when(core == 1)(lambda: run(1))


LATE_ROUNDS = (
    (
        ("p1", "p-1", "p-3", "b5", "b3", "G4", "t1", "t-1", "G3",),
        ("b1", "G2",),
        ("b-1", "G1",),
        ("g-3", "G0",),
    ),
    (
        ("p5", "p7", "p9", "p11", "b1", "b3", "t5", "t7", "G0",),
        ("b5", "G1",),
        ("b7", "G2",),
        ("g9", "G3",),
        ("g11", "G4",),
    ),
)
OWN_NAMES = ("s", "l", "h", "p", "t")
ROWS_TYPE = pltpu.VMEM((ROWS, BLK, SLOTS * BLK), jnp.bfloat16)


def vmem_call(kernel, operands, out_shape, name):
    vmem = pl.BlockSpec(memory_space=pltpu.VMEM)
    return pl.pallas_call(
        kernel,
        out_shape=out_shape,
        in_specs=[vmem] * len(operands),
        out_specs=(vmem,) * len(out_shape),
        compiler_params=pltpu.CompilerParams(vmem_limit_bytes=8 * 1024 * 1024),
        cost_estimate=pl.CostEstimate(flops=1, bytes_accessed=1, transcendentals=0),
        name=name,
    )(*operands)


def partial_type(names):
    count = max(len(partials_of(core, names)) for core in (0, 1))
    return pltpu.VMEM((count * 2 * BLK, LANES), jnp.float32)


def own_kernel(l_ref, s_ref, h_ref, pattern_ref, *outs):
    *outs, partial_ref, mask_ref = outs
    write_mask(pattern_ref, mask_ref)

    def run(core):
        st = Stored(core, [dict(zip(OWN_NAMES, outs))], mask_ref, [partial_ref])
        st.own_rows({"s": s_ref, "l": l_ref, "h": h_ref})
        st.put_groups("pt")
        st.put_partials("p")

    on_core(run)


def compute_own(l_values, s_values, h_values, turned):
    operands = (l_values, s_values, h_values, turned)
    mask = pltpu.VMEM((MASK_ROWS, LANES), jnp.float32)
    out = (*stored_types(OWN_NAMES), partial_type("p"), mask)
    *own, mask = vmem_call(own_kernel, operands, out, "own")
    return own, mask


def early_kernel(chip_a_ref, chip_b_ref, mask_ref, *refs):
    own, own_partial_ref = dict(zip(OWN_NAMES, refs[:5])), refs[5]
    early = dict(zip(NAMES, refs[6:12]))
    partial_ref, kernel_buf = refs[12:]

    def run(core):
        st = Stored(core, [own, early], mask_ref, [own_partial_ref, partial_ref])
        st.unpack(1 - core, (chip_a_ref, chip_b_ref))
        st.put_groups("pt")
        both = [q for q in GROUPS["k"] if phase_of(core, "k", q) == 1]
        for q in both:
            st.put_both(q, kernel_buf)
        for q in GROUPS["g"]:
            if phase_of(core, "g", q) == 1 and q not in both:
                st.put_group("g", q)
        st.put_partials("gk")

    on_core(run)


def compute_early(chip, mask, own):
    out = (*stored_types(NAMES), partial_type("gk"), ROWS_TYPE)
    return vmem_call(early_kernel, (*chip, mask, *own), out, "early")


def late_kernel(cross_ref, mask_ref, *refs):
    own, own_partial_ref = dict(zip(OWN_NAMES, refs[:5])), refs[5]
    early = dict(zip(NAMES, refs[6:12]))
    partial_ref, early_buf, kernel_hbm, gradient_hbm = refs[12:16]
    late = dict(zip(NAMES, refs[16:22]))
    kernel_buf, gradient_buf, sems = refs[22:]

    def run(core):
        st = Stored(core, [own, early, late], mask_ref, [own_partial_ref, partial_ref])
        copies = []

        def send(buf, hbm, first, last):
            for row in range(first, last):
                copy = pltpu.make_async_copy(buf.at[row], hbm.at[row], sems.at[len(copies)])
                copy.start()
                copies.append(copy)

        for q in GROUPS["k"]:
            if phase_of(core, "k", q) < 2:
                send(early_buf, kernel_hbm, max(q, 0), q + 2)
        st.unpack(core, (cross_ref,))
        for steps in LATE_ROUNDS[core]:
            ready = []
            for step in steps:
                name, q = step[0], int(step[1:])
                if name == "G":
                    st.gradient_rows(q, gradient_buf)
                    ready.append((gradient_buf, gradient_hbm, 2 * q, min(2 * q + 2, ROWS)))
                elif name == "b":
                    st.put_both(q, kernel_buf)
                    ready.append((kernel_buf, kernel_hbm, max(q, 0), q + 2))
                else:
                    st.put_group(name, q)
            for item in ready:
                send(*item)
        for copy in copies:
            copy.wait()

    on_core(run)


def compute_late(cross, mask, own, early):
    vmem = pl.BlockSpec(memory_space=pltpu.VMEM)
    hbm = pl.BlockSpec(memory_space=pl.ANY)
    out = jax.ShapeDtypeStruct((ROWS, BLK, SLOTS * BLK), jnp.bfloat16)
    operands = (cross, mask, *own, *early)
    return pl.pallas_call(
        late_kernel,
        out_shape=(out, out),
        in_specs=[vmem] * len(operands),
        out_specs=(hbm, hbm),
        scratch_shapes=[
            *stored_types(NAMES),
            ROWS_TYPE,
            ROWS_TYPE,
            pltpu.SemaphoreType.DMA((2 * ROWS,)),
        ],
        compiler_params=pltpu.CompilerParams(vmem_limit_bytes=16 * 1024 * 1024),
        name="late",
    )(*operands)


def shards(l_values, s_values, h_values, pattern):
    count = lax.axis_size(AXES)
    cross_pairs, chip_pairs = [], []
    for i in range(0, count, 2):
        j = (i - 1) % count
        cross_pairs += [(i, j), (j, i)]
        chip_pairs += [(i, i + 1), (i + 1, i)]
    cross_out = pack_cross(l_values, s_values, h_values)
    cross = lax.ppermute(cross_out, AXES, cross_pairs)
    chip_out = pack_chip(l_values, s_values, h_values, cross_out)
    chip = [lax.ppermute(part, AXES, chip_pairs) for part in chip_out]
    own, mask = compute_own(l_values, s_values, h_values, pattern.T)
    early = compute_early(chip, mask, own)
    return compute_late(cross, mask, own, early)


def solution(mesh):
    rows = P(AXES, None, None)
    return jax.shard_map(
        shards,
        mesh=mesh,
        in_specs=(rows, rows, rows, P()),
        out_specs=(rows, rows),
        check_vma=False,
    )
```

```python
import functools

import jax
import jax.numpy as jnp
from jax import lax
from jax.experimental import pallas as pl
from jax.experimental.pallas import tpu as pltpu
from jax.sharding import PartitionSpec as P

BLK = 64
SLOTS = 7
REACH = 3
ROWS = 9
LANES = 512
AXES = ("dom", "col")


def shift_of(q):
    return 1 - q % 2


def column_of(q, position):
    return q - REACH + position - shift_of(q)


def halo_plan(side):
    if side == 0:
        rows = {"l": range(-3, 0), "s": range(-6, 0), "h": range(-3, 0)}
    else:
        rows = {"l": range(9, 12), "s": range(9, 15), "h": range(9, 12)}
    full, low, high = [], [], []
    for name in ("s", "l", "h"):
        for q in rows[name]:
            for chunk in range(4):
                need = []
                for position in (2 * chunk, 2 * chunk + 1):
                    slot = position - shift_of(q)
                    column = column_of(q, position)
                    inside = 0 <= slot < SLOTS
                    if name != "l":
                        inside = inside and (column >= -3 if side == 0 else column <= 11)
                    need.append(inside)
                a, b = (name, q, 2 * chunk), (name, q, 2 * chunk + 1)
                if all(need):
                    full.append((a, b))
                elif need[0]:
                    low.append(a)
                elif need[1]:
                    high.append(b)
    while low and high:
        full.append((low.pop(), high.pop()))
    rest = low + high
    while rest:
        a = rest.pop()
        full.append((a, rest.pop() if rest else None))
    return full


PLANS = (halo_plan(0), halo_plan(1))
CHUNKS = len(PLANS[0])
PACKED = CHUNKS * BLK - BLK // 2
CHIP_PARTS = (CHUNKS // 2 * BLK, PACKED - CHUNKS // 2 * BLK)
MASK_FIRST, MASK_ROWS = -6, 22


def write_halo(side, block, out_refs):
    for n, (a, b) in enumerate(PLANS[side]):
        ref, row, lane = block(*a)
        if b is None:
            only = ref[row, :, lane : lane + BLK]
            chunk = jnp.concatenate([only[: BLK // 2], only[BLK // 2 :]], axis=1)
        elif a[:2] == b[:2] and b[2] == a[2] + 1:
            chunk = ref[row, :, lane : lane + 2 * BLK]
        else:
            first = ref[row, :, lane : lane + BLK]
            ref, row, lane = block(*b)
            second = ref[row, :, lane : lane + BLK]
            chunk = jnp.concatenate([first, second], axis=1)
        place = n * BLK
        for out_ref in out_refs:
            if place < out_ref.shape[0]:
                break
            place -= out_ref.shape[0]
        out_ref[place : place + chunk.shape[0], :] = chunk


def sender_block(refs, side, first):
    def block(name, q, position):
        row = q - ROWS if side == 1 else q + ROWS
        return refs[name], row - first[name], (position - shift_of(q)) * BLK

    return block


def pack_cross_kernel(l_hbm, s_hbm, h_hbm, out_ref, l_buf, s_buf, h_buf, sems):
    core = lax.rem(lax.axis_index("col"), 2)
    copies = [
        pltpu.make_async_copy(s_hbm.at[pl.ds(3 * core, 6)], s_buf, sems.at[0]),
        pltpu.make_async_copy(l_hbm.at[pl.ds(6 * core, 3)], l_buf, sems.at[1]),
        pltpu.make_async_copy(h_hbm.at[pl.ds(6 * core, 3)], h_buf, sems.at[2]),
    ]
    for copy in copies:
        copy.start()
    bufs = {"l": l_buf, "s": s_buf, "h": h_buf}
    last = sender_block(bufs, 0, {"l": 6, "s": 3, "h": 6})
    first = sender_block(bufs, 1, {"l": 0, "s": 0, "h": 0})
    for copy in copies:
        copy.wait()
    pl.when(core == 1)(lambda: write_halo(0, last, (out_ref,)))
    pl.when(core == 0)(lambda: write_halo(1, first, (out_ref,)))


def pack_cross(l_values, s_values, h_values):
    hbm = pl.BlockSpec(memory_space=pltpu.HBM)
    return pl.pallas_call(
        pack_cross_kernel,
        out_shape=pltpu.VMEM((PACKED, 128), jnp.bfloat16),
        in_specs=[hbm] * 3,
        out_specs=pl.BlockSpec(memory_space=pltpu.VMEM),
        scratch_shapes=[
            pltpu.VMEM((3, BLK, SLOTS * BLK), jnp.bfloat16),
            pltpu.VMEM((6, BLK, SLOTS * BLK), jnp.bfloat16),
            pltpu.VMEM((3, BLK, SLOTS * BLK), jnp.bfloat16),
            pltpu.SemaphoreType.DMA((3,)),
        ],
        cost_estimate=pl.CostEstimate(flops=1, bytes_accessed=1, transcendentals=0),
        name="pack_cross",
    )(l_values, s_values, h_values)


def write_mask(pattern_ref, mask_ref):
    count, total = mask_ref.shape[0], pattern_ref.shape[1]
    device = lax.axis_index("dom") * lax.axis_size("col") + lax.axis_index("col")
    first = device * ROWS + MASK_FIRST + total
    wanted = lax.rem(first + lax.broadcasted_iota(jnp.int32, (count, total), 0), total)
    index = lax.broadcasted_iota(jnp.int32, (count, total), 1)
    picked = (wanted == index).astype(jnp.float32).astype(jnp.bfloat16)
    pattern = pattern_ref[...].astype(jnp.float32).astype(jnp.bfloat16)
    near = lax.dot_general(
        picked, pattern, (((1,), (1,)), ((), ())), preferred_element_type=jnp.float32
    )
    even = lax.rem(lax.broadcasted_iota(jnp.int32, (count, 1), 0), 2) == 0
    zero = jnp.zeros((count, 1), jnp.float32)
    slots = [zero] + [near[:, s : s + 1] for s in range(SLOTS)] + [zero]
    places = [jnp.where(even, slots[p], slots[p + 1]) for p in range(8)]
    low = lax.broadcasted_iota(jnp.int32, (count, 128), 1) < BLK
    for chunk in range(4):
        mask_ref[:, chunk * 128 : (chunk + 1) * 128] = jnp.where(
            low, places[2 * chunk], places[2 * chunk + 1]
        )


def pack_chip_kernel(l_ref, s_ref, h_ref, after_ref, *out_refs):
    del after_ref
    core = lax.rem(lax.axis_index("col"), 2)
    refs = {"l": l_ref, "s": s_ref, "h": h_ref}
    whole = {"l": 0, "s": 0, "h": 0}
    pl.when(core == 0)(lambda: write_halo(0, sender_block(refs, 0, whole), out_refs))
    pl.when(core == 1)(lambda: write_halo(1, sender_block(refs, 1, whole), out_refs))


def pack_chip(l_values, s_values, h_values, after):
    vmem = pl.BlockSpec(memory_space=pltpu.VMEM)
    return pl.pallas_call(
        pack_chip_kernel,
        out_shape=tuple(pltpu.VMEM((n, 128), jnp.bfloat16) for n in CHIP_PARTS),
        in_specs=[vmem] * 4,
        out_specs=(vmem,) * len(CHIP_PARTS),
        compiler_params=pltpu.CompilerParams(vmem_limit_bytes=8 * 1024 * 1024),
        cost_estimate=pl.CostEstimate(flops=1, bytes_accessed=1, transcendentals=0),
        name="pack_chip",
    )(l_values, s_values, h_values, after)


NAMES = ("s", "l", "h", "p", "t", "g")
RANGE = {"s": (-6, 16), "l": (-4, 13), "h": (-3, 13), "p": (-4, 13), "t": (-1, 9), "g": (-3, 13)}
FACTORS = {"p": ("l", "s"), "t": ("p", "l"), "g": ("h", "p"), "k": ("t", "p")}
GROUPS = {"p": range(-3, 13, 2), "t": range(-1, 9, 2), "g": range(-3, 13, 2), "k": range(-1, 9, 2)}
OFFSET = (-2, -1, -1, 0, 0, 1, 1, 2)
HALVES = ((0, 2), (2, 4))
PIECES = {
    ("p", -3): ((1, 2), (2, 4)),
    ("p", 9): ((0, 2), (2, 3)),
    ("p", 11): ((0, 2),),
    ("g", -3): ((3, 4),),
    ("g", 9): ((0, 2),),
    ("g", 11): ((0, 1),),
}
DEPTH = {("g", -3): (1, 4), ("g", 9): (0, 3), ("g", 11): (0, 2)}
SINGLE = {("t", -1): (1,), ("k", -1): (1,), ("p", 11): (0,), ("g", 11): (0,)}
HALO = (
    {"s": range(-6, 0), "l": range(-3, 0), "h": range(-3, 0)},
    {"s": range(9, 15), "l": range(9, 12), "h": range(9, 12)},
)
ZERO_ROWS = ((("l", -4), ("p", -4)), (("s", 15), ("l", 12), ("h", 12)))
ZERO_CHUNKS = (((-3, 0),), ((9, 3), (11, 2), (11, 3)))


@functools.cache
def phase_of(core, name, q):
    if name in ("s", "l", "h") or q < -3:
        if 0 <= q < ROWS:
            return 0
        return 2 if (q < 0) == (core == 0) else 1
    group = q if q % 2 else q - 1
    left, right = FACTORS[name]
    first, last = DEPTH.get((name, group), (0, 4))
    rows = range(group - REACH + 2 * first, group - REACH + 2 * last)
    return max(
        [phase_of(core, left, group + k) for k in (0, 1)]
        + [phase_of(core, right, m) for m in rows]
    )


@functools.cache
def early_pairs(core, name, q):
    left, right = FACTORS[name]
    if name == "g" and q in GROUPS["k"] and early_pairs(core, "k", q) is None:
        return None
    if phase_of(core, name, q) < 2 or max(phase_of(core, left, q + k) for k in (0, 1)) == 2:
        return None
    first, last = DEPTH.get((name, q), (0, 4))
    pairs = [
        a
        for a in range(first, last)
        if max(phase_of(core, right, q - REACH + 2 * a + k) for k in (0, 1)) < 2
    ]
    if not pairs or (pairs[0] != first and pairs[-1] != last - 1):
        return None
    return pairs[0], pairs[-1] + 1


def partials_of(core, names):
    return [(name, q) for name in names for q in GROUPS[name] if early_pairs(core, name, q)]


def rows_of(name, q, count=1):
    first = (q - RANGE[name][0]) * BLK
    return slice(first, first + count * BLK)


class Stored:
    def __init__(self, core, arrays, mask_ref, partial_refs):
        self.core, self.arrays, self.mask_ref = core, arrays, mask_ref
        self.partial_refs = dict(zip(("p", "gk"), partial_refs))
        self.phase = len(arrays) - 1

    def get(self, name, q, first=0, last=4):
        ref = self.arrays[phase_of(self.core, name, q)][name]
        return ref[rows_of(name, q), first * 128 : last * 128]

    def put(self, name, q, values, first=0, last=4, count=1):
        ref = self.arrays[self.phase][name]
        ref[rows_of(name, q, count), first * 128 : last * 128] = values

    def mask(self, q, first, last):
        row = q - MASK_FIRST
        return self.mask_ref[row : row + 1, first * 128 : last * 128].astype(jnp.bfloat16)

    def pair_mask(self, name, q, first, last):
        shape = (BLK, (last - first) * 128)
        return jnp.concatenate(
            [
                jnp.broadcast_to(self.mask(q + k, first, last), shape)
                for k in SINGLE.get((name, q), (0, 1))
            ],
            axis=0,
        )

    def own_rows(self, refs):
        pad = jnp.zeros((BLK, BLK), jnp.bfloat16)
        for name, ref in refs.items():
            for q in range(ROWS):
                values = ref[q]
                parts = [pad, values] if shift_of(q) else [values, pad]
                stored = jnp.concatenate(parts, axis=1)
                self.put(name, q, stored * self.mask(q, 0, 4))

    def unpack(self, side, refs):
        pad = jnp.zeros((BLK, BLK), jnp.bfloat16)
        content = {}
        for n, keys in enumerate(PLANS[side]):
            for half, key in enumerate(keys):
                if key is not None:
                    content[key] = (n, half)

        def piece(n, first, last):
            place = n * BLK
            for ref in refs:
                if place < ref.shape[0]:
                    break
                place -= ref.shape[0]
            if n == CHUNKS - 1:
                halves = ref[place : place + BLK // 2, :]
                return jnp.concatenate([halves[:, :BLK], halves[:, BLK:]], axis=0)
            return ref[place : place + BLK, first * BLK : last * BLK]

        for name, rows in HALO[side].items():
            for q in rows:
                for chunk in range(4):
                    a, b = (content.get((name, q, 2 * chunk + half)) for half in (0, 1))
                    if a is None and b is None:
                        values = jnp.zeros((BLK, 128), jnp.bfloat16)
                    else:
                        if a is not None and b is not None and a[0] == b[0]:
                            values = piece(a[0], 0, 2)
                        else:
                            values = jnp.concatenate(
                                [pad if p is None else piece(p[0], p[1], p[1] + 1) for p in (a, b)],
                                axis=1,
                            )
                        values = values * self.mask(q, chunk, chunk + 1)
                    self.put(name, q, values, chunk, chunk + 1)
        for name, q in ZERO_ROWS[side]:
            self.put(name, q, jnp.zeros((BLK, LANES), jnp.bfloat16))
        for q, chunk in ZERO_CHUNKS[side]:
            zero = jnp.zeros((2 * BLK, 128), jnp.bfloat16)
            self.put("p", q, zero, chunk, chunk + 1, 2)

    def multiply(self, factors, right, q, first, last, pairs):
        lhs = jnp.concatenate([self.get(name, row, *pairs) for name, row in factors], axis=0)
        slabs = []
        for r in range(2 * pairs[0], 2 * pairs[1]):
            parts = []
            for chunk in range(first, last):
                source = chunk - OFFSET[r]
                if 0 <= source < 4:
                    parts.append(self.get(right, q - REACH + r, source, source + 1))
                else:
                    parts.append(jnp.zeros((BLK, 128), jnp.bfloat16))
            slabs.append(jnp.concatenate(parts, axis=1))
        rhs = jnp.concatenate(slabs, axis=0)
        return jnp.dot(lhs, rhs, preferred_element_type=jnp.float32)

    def factors_of(self, name, q):
        return [(FACTORS[name][0], q + k) for k in SINGLE.get((name, q), (0, 1))]

    def product(self, name, q, first, last, pairs):
        right = FACTORS[name][1]
        return self.multiply(self.factors_of(name, q), right, q, first, last, pairs)

    def partial_at(self, name, q):
        names = "p" if name == "p" else "gk"
        place = partials_of(self.core, names).index((name, q)) * 2 * BLK
        return self.partial_refs[names], slice(place, place + 2 * BLK)

    def put_partials(self, names):
        for name, q in partials_of(self.core, names):
            ref, rows = self.partial_at(name, q)
            for first, last in PIECES.get((name, q), HALVES):
                values = self.product(name, q, first, last, early_pairs(self.core, name, q))
                ref[rows, first * 128 : last * 128] = values

    def late_pairs(self, name, q):
        pairs, early = DEPTH.get((name, q), (0, 4)), None
        if self.phase == 2:
            early = early_pairs(self.core, name, q)
        if early:
            pairs = (early[1], pairs[1]) if early[0] == pairs[0] else (pairs[0], early[0])
        return pairs, early is not None

    def add_partial(self, name, q, first, last, values):
        ref, rows = self.partial_at(name, q)
        return values + ref[rows, first * 128 : last * 128]

    def group(self, name, q):
        pairs, partial = self.late_pairs(name, q)
        for first, last in PIECES.get((name, q), HALVES):
            values = self.product(name, q, first, last, pairs)
            if partial:
                values = self.add_partial(name, q, first, last, values)
            yield first, last, values

    def put_piece(self, name, q, first, last, values):
        values = values.astype(jnp.bfloat16) * self.pair_mask(name, q, first, last)
        used = SINGLE.get((name, q), (0, 1))
        self.put(name, q + used[0], values, first, last, len(used))

    def put_group(self, name, q):
        for first, last, values in self.group(name, q):
            self.put_piece(name, q, first, last, values)

    def put_both(self, q, out_ref):
        pairs, partial = self.late_pairs("g", q)
        assert self.late_pairs("k", q) == (pairs, partial)
        factors = self.factors_of("g", q) + self.factors_of("k", q)
        pieces = []
        for first, last in HALVES:
            values = self.multiply(factors, "p", q, first, last, pairs)
            hls, quintic = values[: 2 * BLK], values[2 * BLK :]
            if partial:
                hls = self.add_partial("g", q, first, last, hls)
                quintic = self.add_partial("k", q, first, last, quintic)
            self.put_piece("g", q, first, last, hls)
            pieces.append((first, last, quintic))
        self.kernel_rows(q, out_ref, pieces)

    def put_groups(self, names):
        for name in names:
            for q in GROUPS[name]:
                if phase_of(self.core, name, q) == self.phase:
                    self.put_group(name, q)

    def kernel_rows(self, q, out_ref, pieces):
        values = []
        used = SINGLE.get(("k", q), (0, 1))
        for first, last, quintic in pieces:
            lsl = jnp.concatenate([self.get("t", q + k, first, last) for k in used], axis=0)
            halved = (quintic - 1.5 * lsl.astype(jnp.float32)).astype(jnp.bfloat16)
            values.append(halved * (-2.0 * self.pair_mask("k", q, first, last)))
        values = jnp.concatenate(values, axis=1)
        if len(used) == 2:
            out_ref[q] = values[:BLK, : SLOTS * BLK]
        out_ref[q + 1] = values[-BLK:, BLK:]

    def gradient_rows(self, pair, out_ref):
        rows = [2 * pair + k for k in (0, 1) if 2 * pair + k < ROWS]
        zero = jnp.zeros((BLK, 128), jnp.bfloat16)
        mirrored = {}
        for step in range(-2, 3 if len(rows) == 2 else 2):
            upper = lower = zero
            if step >= -1:
                upper = self.get("g", 2 * (pair + step), 2 - step, 3 - step)
            if step <= 1:
                lower = self.get("g", 2 * (pair + step) + 1, 1 - step, 2 - step)
            mirrored[step] = jnp.transpose(jnp.concatenate([upper, lower], axis=0))
        for k, q in enumerate(rows):
            chunks = []
            for chunk in range(4):
                other = mirrored[chunk - 2 + k][k * BLK : (k + 1) * BLK]
                own = self.get("g", q, chunk, chunk + 1)
                chunks.append((own + other) * self.mask(q, chunk, chunk + 1))
            values = jnp.concatenate(chunks, axis=1)
            out_ref[q] = values[:, : SLOTS * BLK] if k else values[:, BLK:]


def stored_types(names):
    return tuple(
        pltpu.VMEM(((RANGE[name][1] - RANGE[name][0]) * BLK, LANES), jnp.bfloat16)
        for name in names
    )


def on_core(run):
    core = lax.rem(lax.axis_index("col"), 2)
    pl.when(core == 0)(lambda: run(0))
    pl.when(core == 1)(lambda: run(1))


LATE_ROUNDS = (
    (
        ("p1", "p-1", "p-3", "b5", "b3", "G4", "t1", "t-1", "G3",),
        ("b1", "G2",),
        ("b-1", "G1",),
        ("g-3", "G0",),
    ),
    (
        ("p5", "p7", "p9", "p11", "b1", "b3", "t5", "t7", "G0",),
        ("b5", "G1",),
        ("b7", "G2",),
        ("g9", "G3",),
        ("g11", "G4",),
    ),
)
OWN_NAMES = ("s", "l", "h", "p", "t")
ROWS_TYPE = pltpu.VMEM((ROWS, BLK, SLOTS * BLK), jnp.bfloat16)


def vmem_call(kernel, operands, out_shape, name):
    vmem = pl.BlockSpec(memory_space=pltpu.VMEM)
    return pl.pallas_call(
        kernel,
        out_shape=out_shape,
        in_specs=[vmem] * len(operands),
        out_specs=(vmem,) * len(out_shape),
        compiler_params=pltpu.CompilerParams(vmem_limit_bytes=8 * 1024 * 1024),
        cost_estimate=pl.CostEstimate(flops=1, bytes_accessed=1, transcendentals=0),
        name=name,
    )(*operands)


def partial_type(names):
    count = max(len(partials_of(core, names)) for core in (0, 1))
    return pltpu.VMEM((count * 2 * BLK, LANES), jnp.float32)


def own_kernel(l_ref, s_ref, h_ref, pattern_ref, *outs):
    *outs, partial_ref, mask_ref = outs
    write_mask(pattern_ref, mask_ref)

    def run(core):
        st = Stored(core, [dict(zip(OWN_NAMES, outs))], mask_ref, [partial_ref])
        st.own_rows({"s": s_ref, "l": l_ref, "h": h_ref})
        st.put_groups("pt")
        st.put_partials("p")

    on_core(run)


def compute_own(l_values, s_values, h_values, turned):
    operands = (l_values, s_values, h_values, turned)
    mask = pltpu.VMEM((MASK_ROWS, LANES), jnp.float32)
    out = (*stored_types(OWN_NAMES), partial_type("p"), mask)
    *own, mask = vmem_call(own_kernel, operands, out, "own")
    return own, mask


def early_kernel(chip_a_ref, chip_b_ref, mask_ref, *refs):
    own, own_partial_ref = dict(zip(OWN_NAMES, refs[:5])), refs[5]
    early = dict(zip(NAMES, refs[6:12]))
    partial_ref, kernel_buf = refs[12:]

    def run(core):
        st = Stored(core, [own, early], mask_ref, [own_partial_ref, partial_ref])
        st.unpack(1 - core, (chip_a_ref, chip_b_ref))
        st.put_groups("ptg")
        for q in GROUPS["k"]:
            if phase_of(core, "k", q) < 2:
                st.kernel_rows(q, kernel_buf, st.group("k", q))
        st.put_partials("gk")

    on_core(run)


def compute_early(chip, mask, own):
    out = (*stored_types(NAMES), partial_type("gk"), ROWS_TYPE)
    return vmem_call(early_kernel, (*chip, mask, *own), out, "early")


def late_kernel(cross_ref, mask_ref, *refs):
    own, own_partial_ref = dict(zip(OWN_NAMES, refs[:5])), refs[5]
    early = dict(zip(NAMES, refs[6:12]))
    partial_ref, early_buf, kernel_hbm, gradient_hbm = refs[12:16]
    late = dict(zip(NAMES, refs[16:22]))
    kernel_buf, gradient_buf, sems = refs[22:]

    def run(core):
        st = Stored(core, [own, early, late], mask_ref, [own_partial_ref, partial_ref])
        copies = []

        def send(buf, hbm, first, last):
            for row in range(first, last):
                copy = pltpu.make_async_copy(buf.at[row], hbm.at[row], sems.at[len(copies)])
                copy.start()
                copies.append(copy)

        for q in GROUPS["k"]:
            if phase_of(core, "k", q) < 2:
                send(early_buf, kernel_hbm, max(q, 0), q + 2)
        st.unpack(core, (cross_ref,))
        for steps in LATE_ROUNDS[core]:
            ready = []
            for step in steps:
                name, q = step[0], int(step[1:])
                if name == "G":
                    st.gradient_rows(q, gradient_buf)
                    ready.append((gradient_buf, gradient_hbm, 2 * q, min(2 * q + 2, ROWS)))
                elif name == "b":
                    st.put_both(q, kernel_buf)
                    ready.append((kernel_buf, kernel_hbm, max(q, 0), q + 2))
                else:
                    st.put_group(name, q)
            for item in ready:
                send(*item)
        for copy in copies:
            copy.wait()

    on_core(run)


def compute_late(cross, mask, own, early):
    vmem = pl.BlockSpec(memory_space=pltpu.VMEM)
    hbm = pl.BlockSpec(memory_space=pl.ANY)
    out = jax.ShapeDtypeStruct((ROWS, BLK, SLOTS * BLK), jnp.bfloat16)
    operands = (cross, mask, *own, *early)
    return pl.pallas_call(
        late_kernel,
        out_shape=(out, out),
        in_specs=[vmem] * len(operands),
        out_specs=(hbm, hbm),
        scratch_shapes=[
            *stored_types(NAMES),
            ROWS_TYPE,
            ROWS_TYPE,
            pltpu.SemaphoreType.DMA((2 * ROWS,)),
        ],
        compiler_params=pltpu.CompilerParams(vmem_limit_bytes=16 * 1024 * 1024),
        name="late",
    )(*operands)


def shards(l_values, s_values, h_values, pattern):
    count = lax.axis_size(AXES)
    cross_pairs, chip_pairs = [], []
    for i in range(0, count, 2):
        j = (i - 1) % count
        cross_pairs += [(i, j), (j, i)]
        chip_pairs += [(i, i + 1), (i + 1, i)]
    cross_out = pack_cross(l_values, s_values, h_values)
    cross = lax.ppermute(cross_out, AXES, cross_pairs)
    chip_out = pack_chip(l_values, s_values, h_values, cross_out)
    chip = [lax.ppermute(part, AXES, chip_pairs) for part in chip_out]
    own, mask = compute_own(l_values, s_values, h_values, pattern.T)
    early = compute_early(chip, mask, own)
    return compute_late(cross, mask, own, early)


def solution(mesh):
    rows = P(AXES, None, None)
    return jax.shard_map(
        shards,
        mesh=mesh,
        in_specs=(rows, rows, rows, P()),
        out_specs=(rows, rows),
        check_vma=False,
    )
```
